512 devices in a mesh: pt: 64 (over x, y, core), case: 8 (over z).
Axes of the slice: x: 4, y: 8, z: 8, core: 2. Of those that a mesh axis runs over, the one named last changes fastest.
Arguments:
- points: bfloat16 [8, 32768, 256], P('case', 'pt')
- cotangent: bfloat16 [8, 32768, 256], P('case', 'pt'), may hold values from -6 to 6
- to_hilbert: int32 [8, 32768], P('case', 'pt'), may hold values from 0 to 32767, as said below
- from_hilbert: int32 [8, 32768], P('case', 'pt'), may hold values from 0 to 32767, as said below
- ln_gain: float32 [256], replicated, may hold values from 0.1 to 1.9
- ln_bias: float32 [256], replicated, may hold values from -3 to 3
- w_qkv: bfloat16 [256, 768], replicated, may hold values from -0.5 to 0.5
- b_qkv: float32 [768], replicated, may hold values from -3 to 3
- w_out: bfloat16 [256, 256], replicated, may hold values from -0.375 to 0.375
- b_out: float32 [256], replicated, may hold values from -3 to 3
Outputs:
- output: bfloat16 [8, 32768, 256], P('case', 'pt')
- grad_points: bfloat16 [8, 32768, 256], P('case', 'pt')
- grad_w_qkv: float32 [256, 768], replicated
- grad_b_qkv: float32 [768], replicated
- grad_w_out: float32 [256, 256], replicated
- grad_b_out: float32 [256], replicated
- grad_gain: float32 [256], replicated
- grad_bias: float32 [256], replicated
The draws below stay inside these ranges and needn't reach their ends.
Inputs may be any that keep to these rules, and one draw needn't show every extreme that they name: `to_hilbert`: for each slab a permutation. Shard s holds Z positions and Hilbert positions s * 512 to (s + 1) * 512 - 1; every point's Hilbert position lies in its own shard or a neighbouring one, and a point that changes shard lies in the half of its shard nearer to that neighbour in both orders. Across each boundary as many points cross in one direction as in the other, at most 256, and exactly 256 at some boundary of every slab. `from_hilbert`: the inverse permutation of to_hilbert for each slab.
All inputs are finite; a program needn't handle non-finite values.
Results may differ from the reference program's by a relative error of at most 0.005.
The reference program's roundings to bfloat16 on the way count: a program that leaves them out, or rounds other values in their place, can miss the bound.
Values may be sent and summed in bfloat16 or wider, within the bound.
A program may use at most 64 MiB of HBM per device.

```python
import math
import jax
import jax.numpy as jnp
from jax import lax

D = 256
HEADS = 8
HEAD = 32
PATCH = 256
PTS = 512
CAP = 256
POINTS = 32768
CASES = 8


def serial_order(key):
    half_shard = PTS // 2
    blocks = POINTS // PTS - 1

    def one_case(case_key):
        subkeys = jax.random.split(case_key, 6)
        counts = jax.random.randint(subkeys[0], (blocks,), CAP // 4, CAP + 1)
        chosen = jax.random.randint(subkeys[1], (), 0, blocks)
        counts = jnp.where(jnp.arange(blocks) == chosen, CAP, counts)
        left_rank = jax.vmap(lambda item: jax.random.permutation(item, half_shard))(jax.random.split(subkeys[2], blocks))
        right_rank = jax.vmap(lambda item: jax.random.permutation(item, half_shard))(jax.random.split(subkeys[3], blocks))
        ends_right = jnp.concatenate([left_rank < counts[:, None], right_rank >= counts[:, None]], axis=1).astype(jnp.int32)
        shuffle = jax.vmap(lambda item: jax.random.permutation(item, PTS))(jax.random.split(subkeys[4], blocks))
        sorted_items = jnp.argsort(ends_right * PTS + shuffle, axis=1, stable=True)
        positions = jnp.argsort(sorted_items, axis=1, stable=True)
        middle = positions + half_shard + PTS * jnp.arange(blocks)[:, None]
        edge_perms = jax.vmap(lambda item: jax.random.permutation(item, half_shard))(jax.random.split(subkeys[5], 2))
        head_part = edge_perms[0]
        tail_part = edge_perms[1] + POINTS - half_shard
        return jnp.concatenate([head_part, middle.reshape(-1), tail_part]).astype(jnp.int32)
    return jax.vmap(one_case)(jax.random.split(key, CASES))


def draw_to_hilbert(key, part):
    return serial_order(key)


def draw_from_hilbert(key, part):
    ordering = serial_order(key)
    return jnp.argsort(ordering, axis=1, stable=True).astype(jnp.int32)


def draw_points(key, part):
    key = jax.random.fold_in(key, 7)
    subkeys = jax.random.split(key, 3)
    shape = (CASES, POINTS, D)
    drawn_draw = jax.random.normal(subkeys[0], shape, jnp.float32)
    row_scale = jnp.exp(jax.random.uniform(subkeys[1], (CASES, POINTS, 1), jnp.float32, math.log(0.3), math.log(3.0)))
    column_scale = jnp.exp(jax.random.uniform(subkeys[2], (1, 1, D), jnp.float32, math.log(0.3), math.log(3.0)))
    return (drawn_draw * row_scale * column_scale).astype(jnp.bfloat16)


def shard_levels(key, extent, shards, smallest, largest):
    def one(axis_at, shards_of):
        steps = jax.random.uniform(jax.random.fold_in(jax.random.fold_in(key, 6), axis_at), (shards_of,), jnp.float32, smallest / len(shards), largest / len(shards))
        return jnp.repeat(jnp.exp(steps), extent[axis_at] // shards_of).reshape((-1,) + (1,) * (len(extent) - axis_at - 1))

    factor_of = one(*shards[0])
    for cut in shards[1:]:
        factor_of = factor_of * one(*cut)
    return factor_of


def scatter_about(own_key, dims, scale, limit, shards=(), held_as=jnp.bfloat16):
    entries = scale * jax.random.normal(own_key, dims, jnp.float32)
    if shards:
        entries = entries * shard_levels(own_key, dims, shards, -0.22, 0.18)
    return jnp.clip(entries, -limit, limit).astype(held_as)


def setup_inputs(seed: int = 0) -> dict:
    splits = jax.random.split(jax.random.key(seed), 11)
    return {
        "points": draw_points(jax.random.fold_in(splits[10], 71), 0),
        "cotangent": scatter_about(splits[1], (CASES, POINTS, D), 1.0, 6.0, ((0, 8), (1, 64))),
        "to_hilbert": draw_to_hilbert(jax.random.fold_in(splits[10], 71), 0),
        "from_hilbert": draw_from_hilbert(jax.random.fold_in(splits[10], 71), 0),
        "ln_gain": jnp.clip(1.0 + 0.18 * jax.random.normal(splits[4], (D,), jnp.float32), 0.1, 1.9),
        "ln_bias": scatter_about(splits[5], (D,), 0.5, 3.0, (), jnp.float32),
        "w_qkv": scatter_about(splits[6], (D, 3 * D), (D // 2) ** -0.5, 0.5),
        "b_qkv": scatter_about(splits[7], (3 * D,), 0.5, 3.0, (), jnp.float32),
        "w_out": scatter_about(splits[8], (D, D), D ** -0.5, 0.375),
        "b_out": scatter_about(splits[9], (D,), 0.5, 3.0, (), jnp.float32),
    }


epsilon = 1e-05

def patch_block(patch_points, patch_cotangent, ln_gain, ln_bias, w_qkv, b_qkv, w_out, b_out):
    features = patch_points.astype(jnp.float32)
    centered = features - lax.optimization_barrier(jnp.mean(features, axis=-1, keepdims=True))
    inverse_std = lax.rsqrt(lax.optimization_barrier(jnp.mean(centered * centered, axis=-1, keepdims=True)) + epsilon)
    standard = centered * inverse_std
    normed = (standard * ln_gain + ln_bias).astype(jnp.bfloat16)
    projected = (jnp.dot(normed, w_qkv, preferred_element_type=jnp.float32) + b_qkv).astype(jnp.bfloat16)
    triple = projected.reshape(PATCH, 3, HEADS, HEAD).astype(jnp.float32)
    query_rows = triple[:, 0]
    key_rows = triple[:, 1]
    value_rows = triple[:, 2]
    softmax_scale = 1.0 / math.sqrt(HEAD)
    scores = jnp.einsum('qhd,khd->hqk', query_rows, key_rows) * softmax_scale
    exponent = jnp.exp(scores)
    probability = exponent / lax.optimization_barrier(jnp.sum(exponent, axis=-1, keepdims=True))
    weights_low = lax.optimization_barrier(probability.astype(jnp.bfloat16)).astype(jnp.float32)
    attended = jnp.einsum('hqk,khd->qhd', weights_low, value_rows).astype(jnp.bfloat16).reshape(PATCH, D)
    branch = jnp.dot(attended, w_out, preferred_element_type=jnp.float32) + b_out
    result = (features + branch).astype(jnp.bfloat16)
    d_attended = jnp.dot(patch_cotangent, w_out.T, preferred_element_type=jnp.float32).astype(jnp.bfloat16)
    d_heads = lax.optimization_barrier(d_attended).reshape(PATCH, HEADS, HEAD).astype(jnp.float32)
    d_values = jnp.einsum('hqk,qhd->khd', weights_low, d_heads)
    d_prob = jnp.einsum('qhd,khd->hqk', d_heads, value_rows)
    d_scores = probability * (d_prob - lax.optimization_barrier(jnp.sum(probability * d_prob, axis=-1, keepdims=True))) * softmax_scale
    d_low = lax.optimization_barrier(d_scores.astype(jnp.bfloat16)).astype(jnp.float32)
    d_query = jnp.einsum('hqk,khd->qhd', d_low, key_rows)
    d_keys = jnp.einsum('hqk,qhd->khd', d_low, query_rows)
    d_projected = jnp.stack([d_query, d_keys, d_values], axis=1).reshape(PATCH, 3 * D).astype(jnp.bfloat16)
    d_normed = jnp.dot(d_projected, w_qkv.T, preferred_element_type=jnp.float32)
    scaled_grad = d_normed * ln_gain
    d_input = inverse_std * (scaled_grad - lax.optimization_barrier(jnp.mean(scaled_grad, axis=-1, keepdims=True)) - standard * lax.optimization_barrier(jnp.mean(scaled_grad * standard, axis=-1, keepdims=True)))
    grad_rows = (patch_cotangent.astype(jnp.float32) + d_input).astype(jnp.bfloat16)
    weight_terms = (jnp.dot(normed.T, d_projected, preferred_element_type=jnp.float32), lax.optimization_barrier(jnp.sum(d_projected.astype(jnp.float32), axis=0)), jnp.dot(attended.T, patch_cotangent, preferred_element_type=jnp.float32), lax.optimization_barrier(jnp.sum(patch_cotangent.astype(jnp.float32), axis=0)), lax.optimization_barrier(jnp.sum(d_normed * standard, axis=0)), lax.optimization_barrier(jnp.sum(d_normed, axis=0)))
    return (result, grad_rows, weight_terms)

def reference(points, cotangent, to_hilbert, from_hilbert, ln_gain, ln_bias, w_qkv, b_qkv, w_out, b_out):
    hilbert_points = jnp.take_along_axis(points, from_hilbert[:, :, None], axis=1)
    hilbert_cotangent = jnp.take_along_axis(cotangent, from_hilbert[:, :, None], axis=1)
    patch_count = CASES * POINTS // PATCH
    point_patches = hilbert_points.reshape(patch_count, PATCH, D)
    cotangent_patches = hilbert_cotangent.reshape(patch_count, PATCH, D)
    initial = (jnp.zeros((D, 3 * D), jnp.float32), jnp.zeros((3 * D,), jnp.float32), jnp.zeros((D, D), jnp.float32), jnp.zeros((D,), jnp.float32), jnp.zeros((D,), jnp.float32), jnp.zeros((D,), jnp.float32))

    def advance(carry, pair):
        result, grad_rows, weight_terms = patch_block(pair[0], pair[1], ln_gain, ln_bias, w_qkv, b_qkv, w_out, b_out)
        return (tuple((total + term for total, term in zip(carry, weight_terms))), (result, grad_rows))
    sums, (results, gradients) = lax.scan(advance, initial, (point_patches, cotangent_patches))
    hilbert_output = results.reshape(CASES, POINTS, D)
    hilbert_grad = gradients.reshape(CASES, POINTS, D)
    output = jnp.take_along_axis(hilbert_output, to_hilbert[:, :, None], axis=1)
    grad_points = jnp.take_along_axis(hilbert_grad, to_hilbert[:, :, None], axis=1)
    factor = 1.0 / math.sqrt(CASES * POINTS)
    return (output, grad_points, sums[0] * factor, sums[1] * factor, sums[2] * factor, sums[3] * factor, sums[4] * factor, sums[5] * factor)
```

```python
import functools
import math

import jax
import jax.numpy as jnp
from jax import lax
from jax.experimental import pallas as pl
from jax.experimental.pallas import tpu as pltpu
from jax.sharding import PartitionSpec as P

D = 256
HEADS = 8
HEAD = 32
PATCH = 256
LEN = 512
HALF = 256
WIN = 1024
TILES = 32
epsilon = 1e-05
VMEM_LIMIT = 60 * 1024 * 1024
SCALE = 1.0 / math.sqrt(HEAD)
EXP2_SCALE = SCALE * math.log2(math.e)

MESH = pl.DeviceIdType.MESH
F32 = jnp.float32
BF16 = jnp.bfloat16


def nn(a, b):
    return lax.dot_general(a, b, (((1,), (0,)), ((), ())), preferred_element_type=F32)


def nt(a, b):
    return lax.dot_general(a, b, (((1,), (1,)), ((), ())), preferred_element_type=F32)


def one_hot(index_row, low, width):
    columns = [
        jnp.transpose(jnp.broadcast_to(index_row[:, a : a + 128], (128, 128))) for a in (0, 128)
    ]
    column = jnp.concatenate(columns, axis=0) - low
    lane = lax.broadcasted_iota(jnp.int32, (256, 128), 1)
    return jnp.concatenate(
        [jnp.where(column == lane + b, 1.0, 0.0).astype(BF16) for b in range(0, width, 128)],
        axis=1,
    )


def to_tiles(block):
    return jnp.concatenate([block[:, a : a + 128].reshape(16, 16, 128) for a in (0, 128)], axis=0)


def kernel(
    n_pt,
    n_case,
    n_x,
    n_y,
    points,
    cotangent,
    to_hilbert,
    from_hilbert,
    ln_gain,
    ln_bias,
    w_qkv_in,
    b_qkv,
    w_out_in,
    b_out,
    output,
    grad_points,
    sums1,
    sums2,
    to_s,
    from_s,
    gain_s,
    bias_s,
    b_qkv_s,
    b_out_s,
    w_qkv,
    w_out,
    point_win,
    cot_win,
    out_win,
    grad_win,
    hilbert_p,
    hilbert_c,
    standard_s,
    inverse_s,
    normed_s,
    proj_s,
    d_att_s,
    prob_s,
    attended_t_s,
    d_proj_s,
    vector_s,
    acc1,
    acc2,
    core_send1,
    core_send2,
    core_recv1,
    core_recv2,
    x_send1,
    x_send2,
    x_recv1,
    x_recv2,
    y_send1,
    y_send2,
    y_recv1,
    y_recv2,
    z_recv1,
    z_recv2,
    out_stage,
    grad_stage,
    local_sem,
    ex_send,
    ex_recv,
    ar_send,
    ar_recv,
):
    pt = lax.axis_index("pt")
    case = lax.axis_index("case")
    core = lax.rem(pt, 2)
    member = lax.div(pt, 2)
    x_at = lax.div(member, n_y)
    y_at = lax.rem(member, n_y)
    left = lax.rem(pt + n_pt - 1, n_pt)
    right = lax.rem(pt + 1, n_pt)
    sibling = pt + 1 - 2 * core
    outer = lax.rem(pt + n_pt - 1 + 2 * core, n_pt)

    def x_peer(r):
        to = lax.rem(x_at + r, n_x)
        return to, {"pt": (to * n_y + y_at) * 2 + core, "case": case}

    def y_peer(r):
        to = lax.rem(y_at + r, n_y)
        return to, {"pt": (x_at * n_y + to) * 2 + core, "case": case}

    def z_peer(r):
        to = lax.rem(case + r, n_case)
        return to, {"pt": pt, "case": to}

    def for_peers(peer, count, body):
        def step(r, carry):
            body(*peer(r))
            return carry

        lax.fori_loop(1, count, step, 0)

    barrier = pltpu.get_barrier_semaphore()

    def signal(_, where):
        pl.semaphore_signal(barrier, inc=1, device_id=where, device_id_type=MESH)

    to_sib = {"pt": sibling, "case": case}
    signal(None, {"pt": outer, "case": case})
    signal(None, to_sib)
    loads = [
        (points, point_win.at[pl.ds(HALF, LEN)]),
        (cotangent, cot_win.at[pl.ds(HALF, LEN)]),
        (from_hilbert, from_s),
        (ln_gain, gain_s.at[0]),
        (ln_bias, bias_s.at[0]),
        (w_qkv_in, w_qkv),
        (b_qkv, b_qkv_s.at[0]),
        (w_out_in, w_out),
        (b_out, b_out_s.at[0]),
        (to_hilbert, to_s),
    ]
    loads = [pltpu.make_async_copy(a, b, local_sem.at[i]) for i, (a, b) in enumerate(loads)]
    for load in loads:
        load.start()
    for_peers(x_peer, n_x, signal)
    for_peers(y_peer, n_y, signal)
    for_peers(z_peer, n_case, signal)
    pl.semaphore_wait(barrier, 2 + (n_x - 1) + (n_y - 1) + (n_case - 1))

    def remote(src, dst, send_sem, recv_sem, where):
        return pltpu.make_async_remote_copy(
            src_ref=src,
            dst_ref=dst,
            send_sem=send_sem,
            recv_sem=recv_sem,
            device_id=where,
            device_id_type=MESH,
        )

    def to_sides(src, first_row, win, at):
        low = remote(
            src.at[pl.ds(first_row, HALF)],
            win.at[pl.ds(HALF + LEN, HALF)],
            ex_send.at[at],
            ex_recv.at[at],
            {"pt": left, "case": case},
        )
        high = remote(
            src.at[pl.ds(first_row + HALF, HALF)],
            win.at[pl.ds(0, HALF)],
            ex_send.at[at + 1],
            ex_recv.at[at + 1],
            {"pt": right, "case": case},
        )
        low.start()
        high.start()
        return low, high

    ex_p = to_sides(points, 0, point_win, 0)
    ex_c = to_sides(cotangent, 0, cot_win, 2)

    own = pl.ds(HALF, LEN)
    offset = pt * LEN - HALF

    def patch(p):
        return pl.ds(p * PATCH, PATCH)

    for load in loads[:3]:
        load.wait()
    from_row = from_s[...] - offset
    hots = []
    for p in range(2):
        row = from_row[:, p * PATCH : (p + 1) * PATCH]
        hot = one_hot(row, HALF, LEN)
        hilbert_p[patch(p), :] = nn(hot, point_win[own, :])
        hilbert_c[patch(p), :] = nn(hot, cot_win[own, :])
        hots.append(one_hot(row, p * (HALF + LEN), HALF))
    for load in loads[3:]:
        load.wait()

    gain = gain_s[...]
    for p in range(2):
        ex_p[1 - p].wait_recv()
        features = hilbert_p[patch(p), :] + nn(hots[p], point_win[pl.ds(p * (HALF + LEN), HALF), :])
        hilbert_p[patch(p), :] = features
        centered = features - jnp.mean(features, axis=-1, keepdims=True)
        inverse = lax.rsqrt(jnp.mean(centered * centered, axis=-1, keepdims=True) + epsilon)
        standard = centered * inverse
        standard_s[patch(p), :] = standard
        inverse_s[patch(p), :] = jnp.broadcast_to(inverse, (PATCH, 128))
        normed = (standard * gain + bias_s[...]).astype(BF16)
        normed_s[patch(p), :] = normed
        proj_s[patch(p), :] = (nn(normed, w_qkv[...]) + b_qkv_s[...]).astype(BF16)
    for p in range(2):
        ex_c[1 - p].wait_recv()
        cot = hilbert_c[patch(p), :] + nn(hots[p], cot_win[pl.ds(p * (HALF + LEN), HALF), :])
        hilbert_c[patch(p), :] = cot
        d_att_s[patch(p), :] = nt(cot.astype(BF16), w_out[...]).astype(BF16)

    lane_head = lax.broadcasted_iota(jnp.int32, (1, 128), 1) // HEAD
    masks = [jnp.where(lane_head == h, 1.0, 0.0).astype(BF16) for h in range(4)]

    for p in range(2):
        for block in range(2):
            b0 = block * 128
            q = proj_s[patch(p), pl.ds(b0, 128)]
            k = proj_s[patch(p), pl.ds(256 + b0, 128)]
            v_t = jnp.transpose(proj_s[patch(p), pl.ds(512 + b0, 128)])
            da = d_att_s[patch(p), pl.ds(b0, 128)]
            d_v = None
            for h in range(4):
                mask = masks[h]
                exponent = jnp.exp2(nt(k * mask, q) * EXP2_SCALE)
                total = jnp.sum(exponent, axis=0, keepdims=True)
                prob = exponent * (1.0 / total)
                prob_s[(p * 2 + block) * 4 + h] = prob
                prob_low = prob.astype(BF16)
                att_t = nn(v_t[h * HEAD : (h + 1) * HEAD], prob_low)
                attended_t_s[pl.ds(b0 + h * HEAD, HEAD), patch(p)] = att_t.astype(BF16)
                d_v_h = nn(prob_low, da * mask)
                d_v = d_v_h if d_v is None else d_v + d_v_h
            d_proj_s[patch(p), pl.ds(512 + b0, 128)] = d_v.astype(BF16)

    chunks = (
        (acc1, core_send1, core_recv1, x_send1, x_recv1, y_send1, y_recv1, z_recv1, sums1),
        (acc2, core_send2, core_recv2, x_send2, x_recv2, y_send2, y_recv2, z_recv2, sums2),
    )
    per_x = TILES // n_x
    per_y = per_x // n_y

    def sem(chunk, stage):
        return ar_send.at[chunk * 7 + stage], ar_recv.at[chunk * 7 + stage]

    def wait_total(ref, semaphore):
        pltpu.make_async_copy(ref, ref, semaphore).wait()

    def high_low(value):
        high = value.astype(BF16)
        low = (value - high.astype(F32)).astype(BF16)
        return jnp.concatenate([high, low], axis=0)

    def joined(tile):
        tile = tile.astype(F32)
        return tile[:8] + tile[8:]

    def core_start(chunk, first, second):
        acc, send, recv = chunks[chunk][:3]
        acc[0] = to_tiles(first)
        acc[1] = to_tiles(second)
        send[pl.ds(0, TILES)] = acc[1 - core].astype(BF16)
        if chunk:
            theirs = pl.multiple_of((1 - core) * 8, 8)
            send[TILES] = high_low(vector_s[pl.ds(theirs, 8), :])
        copy = remote(send, recv, *sem(chunk, 0), to_sib)
        copy.start()
        return copy

    def x_start(chunk, copy):
        acc, _, recv0, send, recv = chunks[chunk][:5]
        copy.wait()
        half = (acc[core] + recv0[pl.ds(0, TILES)].astype(F32)).astype(BF16)
        send[:, pl.ds(0, per_x)] = half.reshape(n_x, per_x, 16, 128)
        if chunk:
            mine = pl.multiple_of(core * 8, 8)
            tile = high_low(vector_s[pl.ds(mine, 8), :] + joined(recv0[TILES]))
            for i in range(n_x):
                send[i, per_x] = tile
        recv[pl.ds(x_at, 1)] = send[pl.ds(x_at, 1)]
        s, r = sem(chunk, 1)
        for_peers(
            x_peer,
            n_x,
            lambda to, where: remote(send.at[to], recv.at[x_at], s, r, where).start(),
        )

    def y_start(chunk):
        recv0, send, recv = chunks[chunk][4:7]
        wait_total(recv0.at[pl.ds(0, n_x - 1)], sem(chunk, 1)[1])
        part = jnp.sum(recv0[:, pl.ds(0, per_x)].astype(F32), axis=0).astype(BF16)
        send[:, pl.ds(0, per_y)] = part.reshape(n_y, per_y, 16, 128)
        if chunk:
            total = joined(recv0[0, per_x])
            for i in range(1, n_x):
                total = total + joined(recv0[i, per_x])
            tile = high_low(total)
            for i in range(n_y):
                send[i, per_y] = tile
        recv[pl.ds(y_at, 1)] = send[pl.ds(y_at, 1)]
        s, r = sem(chunk, 2)
        for_peers(
            y_peer,
            n_y,
            lambda to, where: remote(send.at[to], recv.at[y_at], s, r, where).start(),
        )

    def z_start(chunk):
        recv0, recv = chunks[chunk][6:8]
        wait_total(recv0.at[pl.ds(0, n_y - 1)], sem(chunk, 2)[1])
        part = jnp.sum(recv0[:, pl.ds(0, per_y)].astype(F32), axis=0).astype(BF16)
        recv[case, pl.ds(0, per_y)] = part
        if chunk:
            total = joined(recv0[0, per_y])
            for i in range(1, n_y):
                total = total + joined(recv0[i, per_y])
            recv[case, per_y] = high_low(total)
        s, r = sem(chunk, 3)
        slot = recv.at[case]
        for_peers(z_peer, n_case, lambda to, where: remote(slot, slot, s, r, where).start())

    def y_back(chunk):
        recv0, result = chunks[chunk][7:9]
        wait_total(recv0.at[pl.ds(0, n_case - 1)], sem(chunk, 3)[1])
        at = pl.ds(x_at * per_x + y_at * per_y, per_y)
        result[core, at] = jnp.sum(recv0[:, pl.ds(0, per_y)].astype(F32), axis=0).astype(BF16)
        if chunk:
            total = joined(recv0[0, per_y])
            for i in range(1, n_case):
                total = total + joined(recv0[i, per_y])
            result[core, TILES] = high_low(total)
        s, r = sem(chunk, 4)
        slot = result.at[core, at]
        for_peers(y_peer, n_y, lambda to, where: remote(slot, slot, s, r, where).start())

    def x_back(chunk):
        result = chunks[chunk][8]
        wait_total(result.at[core, pl.ds(0, (n_y - 1) * per_y)], sem(chunk, 4)[1])
        s, r = sem(chunk, 5)
        slot = result.at[core, pl.ds(x_at * per_x, per_x)]
        for_peers(x_peer, n_x, lambda to, where: remote(slot, slot, s, r, where).start())

    def core_back(chunk):
        result = chunks[chunk][8]
        wait_total(result.at[core, pl.ds(0, (n_x - 1) * per_x)], sem(chunk, 5)[1])
        slot = result.at[core]
        copy = remote(slot, slot, *sem(chunk, 6), to_sib)
        copy.start()
        return copy

    def finish(chunk, copy):
        _, _, _, send1, _, send2, _, recv3, result = chunks[chunk]
        wait_total(send1.at[pl.ds(0, n_x - 1)], sem(chunk, 1)[0])
        wait_total(send2.at[pl.ds(0, n_y - 1)], sem(chunk, 2)[0])
        wait_total(recv3.at[pl.ds(0, n_case - 1)], sem(chunk, 3)[0])
        wait_total(result.at[core, pl.ds(0, (n_y - 1) * per_y)], sem(chunk, 4)[0])
        wait_total(result.at[core, pl.ds(0, (n_x - 1) * per_x)], sem(chunk, 5)[0])
        copy.wait()

    normed_t = jnp.transpose(normed_s[...])
    cot_low = hilbert_c[...].astype(BF16)
    core_copy1 = core_start(
        0, nn(normed_t, d_proj_s[:, pl.ds(512, 256)]), nn(attended_t_s[...], cot_low)
    )

    for p in range(2):
        attended = jnp.transpose(attended_t_s[:, patch(p)])
        branch = nn(attended, w_out[...]) + b_out_s[...]
        out_win[pl.ds(HALF + p * PATCH, PATCH), :] = (hilbert_p[patch(p), :] + branch).astype(BF16)
    ex_out = to_sides(out_win, HALF, out_win, 4)

    for p in range(2):
        for block in range(2):
            b0 = block * 128
            q = proj_s[patch(p), pl.ds(b0, 128)]
            k_t = jnp.transpose(proj_s[patch(p), pl.ds(256 + b0, 128)])
            v = proj_s[patch(p), pl.ds(512 + b0, 128)]
            da = d_att_s[patch(p), pl.ds(b0, 128)]
            d_q_t = []
            d_k = None
            for h in range(4):
                mask = masks[h]
                prob = prob_s[(p * 2 + block) * 4 + h]
                d_prob = nt(v * mask, da)
                row_sum = jnp.sum(prob * d_prob, axis=0, keepdims=True)
                d_s = (prob * (d_prob - row_sum) * SCALE).astype(BF16)
                d_k_h = nn(d_s, q * mask)
                d_k = d_k_h if d_k is None else d_k + d_k_h
                d_q_t.append(nn(k_t[h * HEAD : (h + 1) * HEAD], d_s))
            d_q = jnp.transpose(jnp.concatenate(d_q_t, axis=0))
            d_proj_s[patch(p), pl.ds(b0, 128)] = d_q.astype(BF16)
            d_proj_s[patch(p), pl.ds(256 + b0, 128)] = d_k.astype(BF16)
        if p == 0:
            x_start(0, core_copy1)
        else:
            y_start(0)

    d_proj = d_proj_s[...]
    d_normed = nt(d_proj, w_qkv[...])
    standard = standard_s[...]
    cot_all = hilbert_c[...]
    vector_s[...] = jnp.zeros((16, 128), F32)
    b_sum = jnp.sum(d_proj.astype(F32), axis=0, keepdims=True)
    for part in range(6):
        vector_s[part : part + 1, :] = b_sum[:, part * 128 : part * 128 + 128]
    rest = (
        jnp.sum(cot_all, axis=0, keepdims=True),
        jnp.sum(d_normed * standard, axis=0, keepdims=True),
        jnp.sum(d_normed, axis=0, keepdims=True),
    )
    for i, value in enumerate(rest):
        for part in range(2):
            vector_s[8 + 2 * i + part : 9 + 2 * i + part, :] = value[:, part * 128 : part * 128 + 128]
    core_copy2 = core_start(1, nn(normed_t, d_proj[:, :256]), nn(normed_t, d_proj[:, 256:512]))

    scaled = d_normed * gain
    inverse = inverse_s[...]
    inverse = jnp.concatenate([inverse, inverse], axis=1)
    d_input = inverse * (
        scaled
        - jnp.mean(scaled, axis=-1, keepdims=True)
        - standard * jnp.mean(scaled * standard, axis=-1, keepdims=True)
    )
    grad_win[own, :] = (cot_all + d_input).astype(BF16)
    ex_grad = to_sides(grad_win, HALF, grad_win, 6)

    to_row = to_s[...] - offset

    def to_z_order(pair, win, stage, result, at):
        for copy in pair:
            copy.wait_recv()
        for p in range(2):
            hot = one_hot(to_row[:, p * PATCH : (p + 1) * PATCH], p * HALF, HALF + LEN)
            stage[patch(p), :] = nn(hot, win[pl.ds(p * HALF, HALF + LEN), :]).astype(BF16)
        store = pltpu.make_async_copy(stage, result, local_sem.at[at])
        store.start()
        return store

    x_start(1, core_copy2)
    z_start(0)
    store_out = to_z_order(ex_out, out_win, out_stage, output, 10)
    y_start(1)
    y_back(0)
    store_grad = to_z_order(ex_grad, grad_win, grad_stage, grad_points, 11)
    z_start(1)
    x_back(0)
    y_back(1)
    last1 = core_back(0)
    x_back(1)
    last2 = core_back(1)
    finish(0, last1)
    for pair in (ex_p, ex_c, ex_out, ex_grad):
        for copy in pair:
            copy.wait_send()
    store_out.wait()
    store_grad.wait()
    finish(1, last2)


def results_kernel(
    factor,
    output_in,
    grad_in,
    sums1,
    sums2,
    output,
    grad_points,
    grad_w_qkv,
    grad_b_qkv,
    grad_w_out,
    grad_b_out,
    grad_gain,
    grad_bias,
    vec_s,
    sems,
):
    copies = [
        pltpu.make_async_copy(output_in, output, sems.at[0]),
        pltpu.make_async_copy(grad_in, grad_points, sems.at[1]),
    ]
    for copy in copies:
        copy.start()
    vectors = []
    for c in range(2):
        tile = sums2[c, TILES].astype(F32)
        vectors.append((tile[:8] + tile[8:]) * factor)
    for part in range(6):
        vec_s[0:1, part * 128 : part * 128 + 128] = vectors[0][part : part + 1]
        row = 1 + part // 2
        vec_s[row : row + 1, (part % 2) * 128 : (part % 2) * 128 + 128] = vectors[1][part : part + 1]
    small = [
        pltpu.make_async_copy(vec_s.at[0], grad_b_qkv, sems.at[2]),
        pltpu.make_async_copy(vec_s.at[1, pl.ds(0, D)], grad_b_out, sems.at[3]),
        pltpu.make_async_copy(vec_s.at[2, pl.ds(0, D)], grad_gain, sems.at[4]),
        pltpu.make_async_copy(vec_s.at[3, pl.ds(0, D)], grad_bias, sems.at[5]),
    ]
    for copy in small:
        copy.start()

    def block(sums, c, half):
        return sums[c, pl.ds(half * 16, 16)].reshape(256, 128).astype(F32) * factor

    for half in range(2):
        lanes = half * 128
        grad_w_qkv[:, pl.ds(lanes, 128)] = block(sums2, 0, half)
        grad_w_qkv[:, pl.ds(256 + lanes, 128)] = block(sums2, 1, half)
        grad_w_qkv[:, pl.ds(512 + lanes, 128)] = block(sums1, 0, half)
        grad_w_out[:, pl.ds(lanes, 128)] = block(sums1, 1, half)
    for copy in copies + small:
        copy.wait()


def on_device(n_pt, n_case, n_x, n_y, points, cotangent, to_hilbert, from_hilbert, *params):
    per_x = TILES // n_x
    per_y = per_x // n_y
    vmem = pl.BlockSpec(memory_space=pltpu.VMEM)
    hbm = pl.BlockSpec(memory_space=pl.ANY)
    shape = jax.ShapeDtypeStruct
    rows = shape((LEN, D), BF16)

    def tiles(*lead):
        return pltpu.VMEM((*lead, 16, 128), BF16)

    output, grad_points, sums1, sums2 = pl.pallas_call(
        functools.partial(kernel, n_pt, n_case, n_x, n_y),
        out_shape=(
            rows,
            rows,
            shape((2, TILES, 16, 128), BF16),
            shape((2, TILES + 1, 16, 128), BF16),
        ),
        in_specs=[hbm] * 10,
        out_specs=(hbm, hbm, vmem, vmem),
        scratch_shapes=[
            pltpu.VMEM((1, LEN), jnp.int32),
            pltpu.VMEM((1, LEN), jnp.int32),
            pltpu.VMEM((1, D), F32),
            pltpu.VMEM((1, D), F32),
            pltpu.VMEM((1, 3 * D), F32),
            pltpu.VMEM((1, D), F32),
            pltpu.VMEM((D, 3 * D), BF16),
            pltpu.VMEM((D, D), BF16),
            pltpu.VMEM((WIN, D), BF16),
            pltpu.VMEM((WIN, D), BF16),
            pltpu.VMEM((WIN, D), BF16),
            pltpu.VMEM((WIN, D), BF16),
            pltpu.VMEM((LEN, D), F32),
            pltpu.VMEM((LEN, D), F32),
            pltpu.VMEM((LEN, D), F32),
            pltpu.VMEM((LEN, 128), F32),
            pltpu.VMEM((LEN, D), BF16),
            pltpu.VMEM((LEN, 3 * D), BF16),
            pltpu.VMEM((LEN, D), BF16),
            pltpu.VMEM((16, PATCH, PATCH), F32),
            pltpu.VMEM((D, LEN), BF16),
            pltpu.VMEM((LEN, 3 * D), BF16),
            pltpu.VMEM((16, 128), F32),
            pltpu.VMEM((2, TILES, 16, 128), F32),
            pltpu.VMEM((2, TILES, 16, 128), F32),
            tiles(TILES),
            tiles(TILES + 1),
            tiles(TILES),
            tiles(TILES + 1),
            tiles(n_x, per_x),
            tiles(n_x, per_x + 1),
            tiles(n_x, per_x),
            tiles(n_x, per_x + 1),
            tiles(n_y, per_y),
            tiles(n_y, per_y + 1),
            tiles(n_y, per_y),
            tiles(n_y, per_y + 1),
            tiles(n_case, per_y),
            tiles(n_case, per_y + 1),
            pltpu.VMEM((LEN, D), BF16),
            pltpu.VMEM((LEN, D), BF16),
            pltpu.SemaphoreType.DMA((12,)),
            pltpu.SemaphoreType.DMA((8,)),
            pltpu.SemaphoreType.DMA((8,)),
            pltpu.SemaphoreType.DMA((14,)),
            pltpu.SemaphoreType.DMA((14,)),
        ],
        compiler_params=pltpu.CompilerParams(
            collective_id=0, has_side_effects=True, vmem_limit_bytes=VMEM_LIMIT
        ),
    )(points[0], cotangent[0], to_hilbert, from_hilbert, *params)
    factor = 1.0 / math.sqrt(n_pt * n_case * LEN)
    result = pl.pallas_call(
        functools.partial(results_kernel, factor),
        out_shape=(
            rows,
            rows,
            shape((D, 3 * D), F32),
            shape((3 * D,), F32),
            shape((D, D), F32),
            shape((D,), F32),
            shape((D,), F32),
            shape((D,), F32),
        ),
        in_specs=[vmem] * 4,
        out_specs=(hbm, hbm, vmem, hbm, vmem, hbm, hbm, hbm),
        scratch_shapes=[pltpu.VMEM((4, 3 * D), F32), pltpu.SemaphoreType.DMA((6,))],
        compiler_params=pltpu.CompilerParams(vmem_limit_bytes=VMEM_LIMIT),
    )(output, grad_points, sums1, sums2)
    return (result[0][None], result[1][None], *result[2:])


def solution(mesh):
    n_pt, n_case = mesh.shape["pt"], mesh.shape["case"]
    members = n_pt // 2
    n_y = 8 if members >= 32 else 2
    rows = P("case", "pt", None)
    index = P("case", "pt")
    return jax.shard_map(
        functools.partial(on_device, n_pt, n_case, members // n_y, n_y),
        mesh=mesh,
        in_specs=(rows, rows, index, index) + (P(),) * 6,
        out_specs=(rows, rows) + (P(),) * 6,
        check_vma=False,
    )
```

```python
import functools
import math

import jax
import jax.numpy as jnp
from jax import lax
from jax.experimental import pallas as pl
from jax.experimental.pallas import tpu as pltpu
from jax.sharding import PartitionSpec as P

D = 256
HEADS = 8
HEAD = 32
PATCH = 256
LEN = 512
HALF = 256
WIN = 1024
TILES = 32
epsilon = 1e-05
VMEM_LIMIT = 60 * 1024 * 1024
SCALE = 1.0 / math.sqrt(HEAD)
EXP2_SCALE = SCALE * math.log2(math.e)

MESH = pl.DeviceIdType.MESH
F32 = jnp.float32
BF16 = jnp.bfloat16


def nn(a, b):
    return lax.dot_general(a, b, (((1,), (0,)), ((), ())), preferred_element_type=F32)


def nt(a, b):
    return lax.dot_general(a, b, (((1,), (1,)), ((), ())), preferred_element_type=F32)


def one_hot(index_row, low, width):
    columns = [
        jnp.transpose(jnp.broadcast_to(index_row[:, a : a + 128], (128, 128))) for a in (0, 128)
    ]
    column = jnp.concatenate(columns, axis=0) - low
    lane = lax.broadcasted_iota(jnp.int32, (256, 128), 1)
    return jnp.concatenate(
        [jnp.where(column == lane + b, 1.0, 0.0).astype(BF16) for b in range(0, width, 128)],
        axis=1,
    )


def ring_order(n_x, n_y):
    places = [(x, y) for x in range(n_x) for y in range(n_y) if x or y]
    return sorted(places, key=lambda p: -(min(p[0], n_x - p[0]) + min(p[1], n_y - p[1])))


def to_tiles(block):
    return jnp.concatenate([block[:, a : a + 128].reshape(16, 16, 128) for a in (0, 128)], axis=0)


def kernel(
    n_pt,
    n_case,
    n_x,
    n_y,
    points,
    cotangent,
    to_hilbert,
    from_hilbert,
    ln_gain,
    ln_bias,
    w_qkv_in,
    b_qkv,
    w_out_in,
    b_out,
    output,
    grad_points,
    sums1,
    sums2,
    to_s,
    from_s,
    gain_s,
    bias_s,
    b_qkv_s,
    b_out_s,
    w_qkv,
    w_out,
    point_win,
    cot_win,
    out_win,
    grad_win,
    hilbert_p,
    hilbert_c,
    standard_s,
    inverse_s,
    normed_t_s,
    proj_s,
    d_att_s,
    prob_s,
    attended_t_s,
    d_proj_s,
    d_normed_s,
    vector_s,
    acc1,
    acc2,
    core_send1,
    core_send2,
    core_recv1,
    core_recv2,
    m_send1,
    m_send2,
    m_recv1,
    m_recv2,
    z_recv1,
    z_recv2,
    vec_z,
    vec_m,
    out_stage,
    grad_stage,
    local_sem,
    ex_send,
    ex_recv,
    ar_send,
    ar_recv,
    in_sem,
):
    pt = lax.axis_index("pt")
    case = lax.axis_index("case")
    core = lax.rem(pt, 2)
    members = n_pt // 2
    member = lax.div(pt, 2)
    sibling = pt + 1 - 2 * core
    outer = lax.rem(pt + n_pt - 1 + 2 * core, n_pt)

    x_at = lax.div(member, n_y)
    y_at = lax.rem(member, n_y)

    def m_peer(place):
        to = lax.rem(x_at + place[0], n_x) * n_y + lax.rem(y_at + place[1], n_y)
        return to, {"pt": to * 2 + core, "case": case}

    def z_peer(r):
        to = lax.rem(case + r, n_case)
        return to, {"pt": pt, "case": to}

    m_peers = [m_peer(place) for place in ring_order(n_x, n_y)]
    z_peers = [z_peer(r) for _, r in ring_order(1, n_case)]

    def for_peers(peers, body):
        for peer in peers:
            body(*peer)

    barrier = pltpu.get_barrier_semaphore()

    def signal(_, where):
        pl.semaphore_signal(barrier, inc=1, device_id=where, device_id_type=MESH)

    to_sib = {"pt": sibling, "case": case}
    signal(None, {"pt": outer, "case": case})
    signal(None, to_sib)
    loads = [
        (points, point_win.at[pl.ds(HALF, LEN)]),
        (cotangent, cot_win.at[pl.ds(HALF, LEN)]),
        (from_hilbert, from_s),
        (ln_gain, gain_s.at[0]),
        (ln_bias, bias_s.at[0]),
        (w_qkv_in, w_qkv),
        (b_qkv, b_qkv_s.at[0]),
        (w_out_in, w_out),
        (b_out, b_out_s.at[0]),
        (to_hilbert, to_s),
    ]
    loads = [pltpu.make_async_copy(a, b, local_sem.at[i]) for i, (a, b) in enumerate(loads)]
    for load in loads:
        load.start()
    near = [m_peer((0, 1)), m_peer((0, n_y - 1)), m_peer((1, 0)), m_peer((n_x - 1, 0))]
    near += [z_peer(1), z_peer(n_case - 1)]
    for_peers(near, signal)
    pl.semaphore_wait(barrier, 2 + len(near))

    def tell(step, peers):
        for _, where in peers:
            pl.semaphore_signal(in_sem.at[step], inc=1, device_id=where, device_id_type=MESH)

    def heard(step, peers):
        pl.semaphore_wait(in_sem.at[step], len(peers))

    steps = [near]
    if n_y > 4 or n_case > 4:
        steps.append([m_peer((0, 2)), m_peer((0, n_y - 2)), z_peer(2), z_peer(n_case - 2)])
    steps.append([m_peer((dx, 0)) for dx in range(1, n_x)])
    tell(0, steps[0])

    def remote(src, dst, send_sem, recv_sem, where):
        return pltpu.make_async_remote_copy(
            src_ref=src,
            dst_ref=dst,
            send_sem=send_sem,
            recv_sem=recv_sem,
            device_id=where,
            device_id_type=MESH,
        )

    halves = (1 - core, core)

    def rows_of(p, first=0):
        return pl.ds(pl.multiple_of(first + p * PATCH, PATCH), PATCH)

    def side_rows(p):
        return pl.ds(pl.multiple_of(p * (HALF + LEN), HALF), HALF)

    def to_side(i, src, first_row, win, at):
        where = to_sib if i == 0 else {"pt": outer, "case": case}
        p = halves[i]
        copy = remote(
            src.at[rows_of(p, first_row)],
            win.at[side_rows(1 - p)],
            ex_send.at[at + i],
            ex_recv.at[at + i],
            where,
        )
        copy.start()
        return copy

    ex_p = [to_side(i, points, 0, point_win, 0) for i in (1, 0)][::-1]
    ex_c = [to_side(i, cotangent, 0, cot_win, 2) for i in (1, 0)][::-1]
    ex_out = [None, None]
    ex_grad = [None, None]

    own = pl.ds(HALF, LEN)
    offset = pt * LEN - HALF

    for load in loads[:3]:
        load.wait()
    hots = []
    for i, p in enumerate(halves):
        row = from_s[:, rows_of(p)] - offset
        hot = one_hot(row, HALF, LEN)
        hilbert_p[i] = nn(hot, point_win[own, :])
        hilbert_c[i] = nn(hot, cot_win[own, :])
        hots.append(one_hot(row, p * (HALF + LEN), HALF))
    for load in loads[3:]:
        load.wait()
    heard(0, steps[0])
    tell(1, steps[1])

    def heard_rings():
        if len(steps) == 3:
            heard(1, steps[1])
            tell(2, steps[2])

    gain = gain_s[...]
    lane_head = lax.broadcasted_iota(jnp.int32, (1, 128), 1) // HEAD
    masks = [jnp.where(lane_head == h, 1.0, 0.0).astype(BF16) for h in range(4)]

    def project(i):
        p = halves[i]
        ex_p[i].wait_recv()
        features = hilbert_p[i] + nn(hots[i], point_win[side_rows(p), :])
        hilbert_p[i] = features
        centered = features - jnp.mean(features, axis=-1, keepdims=True)
        inverse = lax.rsqrt(jnp.mean(centered * centered, axis=-1, keepdims=True) + epsilon)
        standard = centered * inverse
        standard_s[i] = standard
        inverse_s[i] = jnp.broadcast_to(inverse, (PATCH, 128))
        normed = (standard * gain + bias_s[...]).astype(BF16)
        normed_t_s[i] = jnp.transpose(normed)
        proj_s[i] = (nn(normed, w_qkv[...]) + b_qkv_s[...]).astype(BF16)
        ex_c[i].wait_recv()
        cot = hilbert_c[i] + nn(hots[i], cot_win[side_rows(p), :])
        hilbert_c[i] = cot
        d_att_s[i] = nt(cot.astype(BF16), w_out[...]).astype(BF16)

    def first_pass(i):
        for block in range(2):
            b0 = block * 128
            q = proj_s[i, :, pl.ds(b0, 128)]
            k = proj_s[i, :, pl.ds(256 + b0, 128)]
            v_t = jnp.transpose(proj_s[i, :, pl.ds(512 + b0, 128)])
            da = d_att_s[i, :, pl.ds(b0, 128)]
            d_v = None
            for h in range(4):
                mask = masks[h]
                exponent = jnp.exp2(nt(k * mask, q) * EXP2_SCALE)
                total = jnp.sum(exponent, axis=0, keepdims=True)
                prob = exponent * (1.0 / total)
                prob_s[block * 4 + h] = prob
                prob_low = prob.astype(BF16)
                att_t = nn(v_t[h * HEAD : (h + 1) * HEAD], prob_low)
                attended_t_s[i, pl.ds(b0 + h * HEAD, HEAD), :] = att_t.astype(BF16)
                d_v_h = nn(prob_low, da * mask)
                d_v = d_v_h if d_v is None else d_v + d_v_h
            d_proj_s[i, :, pl.ds(512 + b0, 128)] = d_v.astype(BF16)

    def block_output(i):
        attended = jnp.transpose(attended_t_s[i])
        branch = nn(attended, w_out[...]) + b_out_s[...]
        out_win[rows_of(halves[i], HALF), :] = (hilbert_p[i] + branch).astype(BF16)
        ex_out[i] = to_side(i, out_win, HALF, out_win, 4)

    def second_pass(i, block):
        b0 = block * 128
        q = proj_s[i, :, pl.ds(b0, 128)]
        k_t = jnp.transpose(proj_s[i, :, pl.ds(256 + b0, 128)])
        v = proj_s[i, :, pl.ds(512 + b0, 128)]
        da = d_att_s[i, :, pl.ds(b0, 128)]
        d_q_t = []
        d_k = None
        for h in range(4):
            mask = masks[h]
            prob = prob_s[block * 4 + h]
            d_prob = nt(v * mask, da)
            row_sum = jnp.sum(prob * d_prob, axis=0, keepdims=True)
            d_s = (prob * (d_prob - row_sum) * SCALE).astype(BF16)
            d_k_h = nn(d_s, q * mask)
            d_k = d_k_h if d_k is None else d_k + d_k_h
            d_q_t.append(nn(k_t[h * HEAD : (h + 1) * HEAD], d_s))
        d_q = jnp.transpose(jnp.concatenate(d_q_t, axis=0))
        d_proj_s[i, :, pl.ds(b0, 128)] = d_q.astype(BF16)
        d_proj_s[i, :, pl.ds(256 + b0, 128)] = d_k.astype(BF16)

    def add(ref, index, value, i):
        ref[index] = value if i == 0 else ref[index] + value

    def forward_terms(i):
        d_v = d_proj_s[i, :, pl.ds(512, 256)]
        add(acc1, 0, to_tiles(nn(normed_t_s[i], d_v)), i)
        add(acc1, 1, to_tiles(nn(attended_t_s[i], hilbert_c[i].astype(BF16))), i)

    def backward_terms(i):
        d_proj = d_proj_s[i]
        d_normed = nt(d_proj, w_qkv[...])
        d_normed_s[...] = d_normed
        sums = (
            (0, jnp.sum(d_proj.astype(F32), axis=0, keepdims=True)),
            (8, jnp.sum(hilbert_c[i], axis=0, keepdims=True)),
            (10, jnp.sum(d_normed * standard_s[i], axis=0, keepdims=True)),
            (12, jnp.sum(d_normed, axis=0, keepdims=True)),
        )
        if i == 0:
            vector_s[...] = jnp.zeros((16, 128), F32)
        for row, value in sums:
            for part in range(value.shape[1] // 128):
                add(
                    vector_s,
                    slice(row + part, row + part + 1),
                    value[:, part * 128 : part * 128 + 128],
                    i,
                )
        add(acc2, 0, to_tiles(nn(normed_t_s[i], d_proj[:, :256])), i)
        add(acc2, 1, to_tiles(nn(normed_t_s[i], d_proj[:, 256:512])), i)

    def norm_backward(i):
        d_normed = d_normed_s[...]
        standard = standard_s[i]
        scaled = d_normed * gain
        inverse = inverse_s[i]
        inverse = jnp.concatenate([inverse, inverse], axis=1)
        d_input = inverse * (
            scaled
            - jnp.mean(scaled, axis=-1, keepdims=True)
            - standard * jnp.mean(scaled * standard, axis=-1, keepdims=True)
        )
        grad_win[rows_of(halves[i], HALF), :] = (hilbert_c[i] + d_input).astype(BF16)
        ex_grad[i] = to_side(i, grad_win, HALF, grad_win, 6)

    chunks = (
        (acc1, core_send1, core_recv1, m_send1, m_recv1, z_recv1, sums1),
        (acc2, core_send2, core_recv2, m_send2, m_recv2, z_recv2, sums2),
    )
    per = TILES // members

    def sem(chunk, stage):
        return ar_send.at[chunk * 5 + stage], ar_recv.at[chunk * 5 + stage]

    def wait_total(ref, semaphore):
        pltpu.make_async_copy(ref, ref, semaphore).wait()

    def high_low(value):
        high = value.astype(BF16)
        low = (value - high.astype(F32)).astype(BF16)
        return jnp.concatenate([high, low], axis=0)

    def joined(tile):
        tile = tile.astype(F32)
        return tile[:8] + tile[8:]

    def core_start(chunk):
        acc, send, recv = chunks[chunk][:3]
        send[pl.ds(0, TILES)] = acc[1 - core].astype(BF16)
        if chunk:
            theirs = pl.multiple_of((1 - core) * 8, 8)
            send[TILES] = high_low(vector_s[pl.ds(theirs, 8), :])
        copy = remote(send, recv, *sem(chunk, 0), to_sib)
        copy.start()
        return copy

    def m_start(chunk, copy):
        acc, _, recv0, send, recv = chunks[chunk][:5]
        if chunk == 0:
            copy.wait()
        half = (acc[core] + recv0[pl.ds(0, TILES)].astype(F32)).astype(BF16)
        send[...] = half.reshape(members, per, 16, 128)
        recv[pl.ds(member, 1)] = send[pl.ds(member, 1)]
        s, r = sem(chunk, 1)
        for_peers(
            m_peers,
            lambda to, where: remote(send.at[to], recv.at[member], s, r, where).start(),
        )

    def z_start(chunk):
        recv0, recv = chunks[chunk][4:6]
        wait_total(recv0.at[pl.ds(0, members - 1)], sem(chunk, 1)[1])
        recv[case] = jnp.sum(recv0[...].astype(F32), axis=0).astype(BF16)
        s, r = sem(chunk, 2)
        slot = recv.at[case]
        for_peers(z_peers, lambda to, where: remote(slot, slot, s, r, where).start())

    def m_back(chunk):
        recv0, result = chunks[chunk][5:7]
        wait_total(recv0.at[pl.ds(0, n_case - 1)], sem(chunk, 2)[1])
        at = pl.ds(member * per, per)
        result[core, at] = jnp.sum(recv0[...].astype(F32), axis=0).astype(BF16)
        s, r = sem(chunk, 3)
        slot = result.at[core, at]
        for_peers(m_peers, lambda to, where: remote(slot, slot, s, r, where).start())

    def core_back(chunk):
        result = chunks[chunk][6]
        wait_total(result.at[core, pl.ds(0, (members - 1) * per)], sem(chunk, 3)[1])
        slot = result.at[core, pl.ds(0, TILES)]
        copy = remote(slot, slot, *sem(chunk, 4), to_sib)
        copy.start()
        return copy

    def vec_z_start(copy):
        copy.wait()
        mine = pl.multiple_of(core * 8, 8)
        vec_z[case] = high_low(vector_s[pl.ds(mine, 8), :] + joined(core_recv2[TILES]))
        slot = vec_z.at[case]
        for_peers(
            z_peers,
            lambda to, where: remote(slot, slot, ar_send.at[10], ar_recv.at[10], where).start(),
        )

    def vec_m_start():
        wait_total(vec_z.at[pl.ds(0, n_case - 1)], ar_recv.at[10])
        total = joined(vec_z[0])
        for i in range(1, n_case):
            total = total + joined(vec_z[i])
        vec_m[member] = high_low(total)
        slot = vec_m.at[member]
        for_peers(
            m_peers,
            lambda to, where: remote(slot, slot, ar_send.at[11], ar_recv.at[11], where).start(),
        )

    def vec_back():
        wait_total(vec_m.at[pl.ds(0, members - 1)], ar_recv.at[11])
        total = vec_m[...].astype(F32)
        total = jnp.sum(total, axis=0)
        sums2[core, TILES] = high_low(total[:8] + total[8:])
        slot = sums2.at[core, TILES]
        copy = remote(slot, slot, ar_send.at[12], ar_recv.at[12], to_sib)
        copy.start()
        return copy

    def finish(chunk, copy):
        send1, _, recv2, result = chunks[chunk][3:7]
        wait_total(send1.at[pl.ds(0, members - 1)], sem(chunk, 1)[0])
        wait_total(recv2.at[pl.ds(0, n_case - 1)], sem(chunk, 2)[0])
        wait_total(result.at[core, pl.ds(0, (members - 1) * per)], sem(chunk, 3)[0])
        copy.wait()

    project(0)
    first_pass(0)
    block_output(0)
    heard_rings()
    second_pass(0, 0)
    second_pass(0, 1)
    forward_terms(0)
    backward_terms(0)
    norm_backward(0)
    project(1)
    heard(len(steps) - 1, steps[-1])
    first_pass(1)
    forward_terms(1)
    core_copy1 = core_start(0)
    block_output(1)
    second_pass(1, 0)
    m_start(0, core_copy1)
    second_pass(1, 1)
    backward_terms(1)
    core_copy2 = core_start(1)
    norm_backward(1)

    def to_z_order(pair, win, stage, result, at):
        for copy in pair:
            copy.wait_recv()
        for p in range(2):
            row = to_s[:, p * PATCH : (p + 1) * PATCH] - offset
            hot = one_hot(row, p * HALF, HALF + LEN)
            at_p = pl.ds(p * PATCH, PATCH)
            stage[at_p, :] = nn(hot, win[pl.ds(p * HALF, HALF + LEN), :]).astype(BF16)
        store = pltpu.make_async_copy(stage, result, local_sem.at[at])
        store.start()
        return store

    vec_z_start(core_copy2)
    m_start(1, None)
    z_start(0)
    store_out = to_z_order(ex_out, out_win, out_stage, output, 10)
    vec_m_start()
    m_back(0)
    z_start(1)
    store_grad = to_z_order(ex_grad, grad_win, grad_stage, grad_points, 11)
    m_back(1)
    last1 = core_back(0)
    vec_last = vec_back()
    last2 = core_back(1)
    finish(0, last1)
    wait_total(vec_z.at[pl.ds(0, n_case - 1)], ar_send.at[10])
    wait_total(vec_m.at[pl.ds(0, members - 1)], ar_send.at[11])
    for pair in (ex_p, ex_c, ex_out, ex_grad):
        for copy in pair:
            copy.wait_send()
    store_out.wait()
    store_grad.wait()
    vec_last.wait()
    finish(1, last2)


def results_kernel(
    factor,
    output_in,
    grad_in,
    sums1,
    sums2,
    output,
    grad_points,
    grad_w_qkv,
    grad_b_qkv,
    grad_w_out,
    grad_b_out,
    grad_gain,
    grad_bias,
    vec_s,
    sems,
):
    copies = [
        pltpu.make_async_copy(output_in, output, sems.at[0]),
        pltpu.make_async_copy(grad_in, grad_points, sems.at[1]),
    ]
    for copy in copies:
        copy.start()
    vectors = []
    for c in range(2):
        tile = sums2[c, TILES].astype(F32)
        vectors.append((tile[:8] + tile[8:]) * factor)
    for part in range(6):
        vec_s[0:1, part * 128 : part * 128 + 128] = vectors[0][part : part + 1]
        row = 1 + part // 2
        vec_s[row : row + 1, (part % 2) * 128 : (part % 2) * 128 + 128] = vectors[1][part : part + 1]
    small = [
        pltpu.make_async_copy(vec_s.at[0], grad_b_qkv, sems.at[2]),
        pltpu.make_async_copy(vec_s.at[1, pl.ds(0, D)], grad_b_out, sems.at[3]),
        pltpu.make_async_copy(vec_s.at[2, pl.ds(0, D)], grad_gain, sems.at[4]),
        pltpu.make_async_copy(vec_s.at[3, pl.ds(0, D)], grad_bias, sems.at[5]),
    ]
    for copy in small:
        copy.start()

    def block(sums, c, half):
        return sums[c, pl.ds(half * 16, 16)].reshape(256, 128).astype(F32) * factor

    for half in range(2):
        lanes = half * 128
        grad_w_qkv[:, pl.ds(lanes, 128)] = block(sums2, 0, half)
        grad_w_qkv[:, pl.ds(256 + lanes, 128)] = block(sums2, 1, half)
        grad_w_qkv[:, pl.ds(512 + lanes, 128)] = block(sums1, 0, half)
        grad_w_out[:, pl.ds(lanes, 128)] = block(sums1, 1, half)
    for copy in copies + small:
        copy.wait()


def on_device(n_pt, n_case, n_x, n_y, points, cotangent, to_hilbert, from_hilbert, *params):
    members = n_pt // 2
    per = TILES // members
    vmem = pl.BlockSpec(memory_space=pltpu.VMEM)
    hbm = pl.BlockSpec(memory_space=pl.ANY)
    shape = jax.ShapeDtypeStruct
    rows = shape((LEN, D), BF16)

    def tiles(*lead):
        return pltpu.VMEM((*lead, 16, 128), BF16)

    output, grad_points, sums1, sums2 = pl.pallas_call(
        functools.partial(kernel, n_pt, n_case, n_x, n_y),
        out_shape=(
            rows,
            rows,
            shape((2, TILES, 16, 128), BF16),
            shape((2, TILES + 1, 16, 128), BF16),
        ),
        in_specs=[hbm] * 10,
        out_specs=(hbm, hbm, vmem, vmem),
        scratch_shapes=[
            pltpu.VMEM((1, LEN), jnp.int32),
            pltpu.VMEM((1, LEN), jnp.int32),
            pltpu.VMEM((1, D), F32),
            pltpu.VMEM((1, D), F32),
            pltpu.VMEM((1, 3 * D), F32),
            pltpu.VMEM((1, D), F32),
            pltpu.VMEM((D, 3 * D), BF16),
            pltpu.VMEM((D, D), BF16),
            pltpu.VMEM((WIN, D), BF16),
            pltpu.VMEM((WIN, D), BF16),
            pltpu.VMEM((WIN, D), BF16),
            pltpu.VMEM((WIN, D), BF16),
            pltpu.VMEM((2, PATCH, D), F32),
            pltpu.VMEM((2, PATCH, D), F32),
            pltpu.VMEM((2, PATCH, D), F32),
            pltpu.VMEM((2, PATCH, 128), F32),
            pltpu.VMEM((2, D, PATCH), BF16),
            pltpu.VMEM((2, PATCH, 3 * D), BF16),
            pltpu.VMEM((2, PATCH, D), BF16),
            pltpu.VMEM((8, PATCH, PATCH), F32),
            pltpu.VMEM((2, D, PATCH), BF16),
            pltpu.VMEM((2, PATCH, 3 * D), BF16),
            pltpu.VMEM((PATCH, D), F32),
            pltpu.VMEM((16, 128), F32),
            pltpu.VMEM((2, TILES, 16, 128), F32),
            pltpu.VMEM((2, TILES, 16, 128), F32),
            tiles(TILES),
            tiles(TILES + 1),
            tiles(TILES),
            tiles(TILES + 1),
            tiles(members, per),
            tiles(members, per),
            tiles(members, per),
            tiles(members, per),
            tiles(n_case, per),
            tiles(n_case, per),
            tiles(n_case),
            tiles(members),
            pltpu.VMEM((LEN, D), BF16),
            pltpu.VMEM((LEN, D), BF16),
            pltpu.SemaphoreType.DMA((12,)),
            pltpu.SemaphoreType.DMA((8,)),
            pltpu.SemaphoreType.DMA((8,)),
            pltpu.SemaphoreType.DMA((14,)),
            pltpu.SemaphoreType.DMA((14,)),
            pltpu.SemaphoreType.REGULAR((3,)),
        ],
        compiler_params=pltpu.CompilerParams(
            collective_id=0, has_side_effects=True, vmem_limit_bytes=VMEM_LIMIT
        ),
    )(points[0], cotangent[0], to_hilbert, from_hilbert, *params)
    factor = 1.0 / math.sqrt(n_pt * n_case * LEN)
    result = pl.pallas_call(
        functools.partial(results_kernel, factor),
        out_shape=(
            rows,
            rows,
            shape((D, 3 * D), F32),
            shape((3 * D,), F32),
            shape((D, D), F32),
            shape((D,), F32),
            shape((D,), F32),
            shape((D,), F32),
        ),
        in_specs=[vmem] * 4,
        out_specs=(hbm, hbm, vmem, hbm, vmem, hbm, hbm, hbm),
        scratch_shapes=[pltpu.VMEM((4, 3 * D), F32), pltpu.SemaphoreType.DMA((6,))],
        compiler_params=pltpu.CompilerParams(vmem_limit_bytes=VMEM_LIMIT),
    )(output, grad_points, sums1, sums2)
    return (result[0][None], result[1][None], *result[2:])


def solution(mesh):
    n_pt, n_case = mesh.shape["pt"], mesh.shape["case"]
    members = n_pt // 2
    n_y = 8 if members >= 32 else 2
    rows = P("case", "pt", None)
    index = P("case", "pt")
    return jax.shard_map(
        functools.partial(on_device, n_pt, n_case, members // n_y, n_y),
        mesh=mesh,
        in_specs=(rows, rows, index, index) + (P(),) * 6,
        out_specs=(rows, rows) + (P(),) * 6,
        check_vma=False,
    )
```

```python
import functools
import math

import jax
import jax.numpy as jnp
from jax import lax
from jax.experimental import pallas as pl
from jax.experimental.pallas import tpu as pltpu
from jax.sharding import PartitionSpec as P

D = 256
HEADS = 8
HEAD = 32
PATCH = 256
LEN = 512
HALF = 256
WIN = 1024
TILES = 32
epsilon = 1e-05
VMEM_LIMIT = 60 * 1024 * 1024
SCALE = 1.0 / math.sqrt(HEAD)
EXP2_SCALE = SCALE * math.log2(math.e)

MESH = pl.DeviceIdType.MESH
F32 = jnp.float32
BF16 = jnp.bfloat16


def nn(a, b):
    return lax.dot_general(a, b, (((1,), (0,)), ((), ())), preferred_element_type=F32)


def nt(a, b):
    return lax.dot_general(a, b, (((1,), (1,)), ((), ())), preferred_element_type=F32)


def one_hot(index_row, low, width):
    columns = [
        jnp.transpose(jnp.broadcast_to(index_row[:, a : a + 128], (128, 128))) for a in (0, 128)
    ]
    column = jnp.concatenate(columns, axis=0) - low
    lane = lax.broadcasted_iota(jnp.int32, (256, 128), 1)
    return jnp.concatenate(
        [jnp.where(column == lane + b, 1.0, 0.0).astype(BF16) for b in range(0, width, 128)],
        axis=1,
    )


def ring_order(n_x, n_y):
    places = [(x, y) for x in range(n_x) for y in range(n_y) if x or y]
    return sorted(places, key=lambda p: -(min(p[0], n_x - p[0]) + min(p[1], n_y - p[1])))


def to_tiles(block):
    return jnp.concatenate([block[:, a : a + 128].reshape(16, 16, 128) for a in (0, 128)], axis=0)


def kernel(
    n_pt,
    n_case,
    n_x,
    n_y,
    points,
    cotangent,
    to_hilbert,
    from_hilbert,
    ln_gain,
    ln_bias,
    w_qkv_in,
    b_qkv,
    w_out_in,
    b_out,
    output,
    grad_points,
    sums1,
    sums2,
    to_s,
    from_s,
    gain_s,
    bias_s,
    b_qkv_s,
    b_out_s,
    w_qkv,
    w_out,
    point_win,
    cot_win,
    out_win,
    grad_win,
    hilbert_p,
    hilbert_c,
    standard_s,
    inverse_s,
    normed_t_s,
    proj_s,
    d_att_s,
    prob_s,
    attended_t_s,
    d_proj_s,
    d_normed_s,
    vector_s,
    acc1,
    acc2,
    core_send1,
    core_send2,
    core_recv1,
    core_recv2,
    m_send1,
    m_send2,
    m_recv1,
    m_recv2,
    z_recv1,
    z_recv2,
    vec_z,
    vec_m,
    out_stage,
    grad_stage,
    local_sem,
    ex_send,
    ex_recv,
    ar_send,
    ar_recv,
    in_sem,
):
    pt = lax.axis_index("pt")
    case = lax.axis_index("case")
    core = lax.rem(pt, 2)
    member = lax.div(pt, 2)
    sibling = pt + 1 - 2 * core
    outer = lax.rem(pt + n_pt - 1 + 2 * core, n_pt)

    x_at = lax.div(member, n_y)
    y_at = lax.rem(member, n_y)

    def m_peer(place):
        to = lax.rem(x_at + place[0], n_x) * n_y + lax.rem(y_at + place[1], n_y)
        return to, {"pt": to * 2 + core, "case": case}

    def z_peer(r):
        to = lax.rem(case + r, n_case)
        return to, {"pt": pt, "case": to}

    def xz_peer(place):
        x_to = lax.rem(x_at + place[0], n_x)
        z_to = lax.rem(case + place[1], n_case)
        return x_to * n_case + z_to, {"pt": (x_to * n_y + y_at) * 2 + core, "case": z_to}

    def y_peer(r):
        to = lax.rem(y_at + r, n_y)
        return to, {"pt": (x_at * n_y + to) * 2 + core, "case": case}

    xy_peers = [m_peer(place) for place in ring_order(n_x, n_y)]
    z_peers = [z_peer(r) for _, r in ring_order(1, n_case)]
    xz_peers = [xz_peer(place) for place in ring_order(n_x, n_case)]
    y_peers = [y_peer(r) for _, r in ring_order(1, n_y)]
    planes = ((member, xy_peers), (x_at * n_case + case, xz_peers))
    lines = ((case, z_peers), (y_at, y_peers))

    def for_peers(peers, body):
        for peer in peers:
            body(*peer)

    barrier = pltpu.get_barrier_semaphore()

    def signal(_, where):
        pl.semaphore_signal(barrier, inc=1, device_id=where, device_id_type=MESH)

    to_sib = {"pt": sibling, "case": case}
    signal(None, {"pt": outer, "case": case})
    signal(None, to_sib)
    loads = [
        (points, point_win.at[pl.ds(HALF, LEN)]),
        (cotangent, cot_win.at[pl.ds(HALF, LEN)]),
        (from_hilbert, from_s),
        (ln_gain, gain_s.at[0]),
        (ln_bias, bias_s.at[0]),
        (w_qkv_in, w_qkv),
        (b_qkv, b_qkv_s.at[0]),
        (w_out_in, w_out),
        (b_out, b_out_s.at[0]),
        (to_hilbert, to_s),
    ]
    loads = [pltpu.make_async_copy(a, b, local_sem.at[i]) for i, (a, b) in enumerate(loads)]
    for load in loads:
        load.start()
    near = [m_peer((0, 1)), m_peer((0, n_y - 1)), m_peer((1, 0)), m_peer((n_x - 1, 0))]
    near += [z_peer(1), z_peer(n_case - 1)]
    for_peers(near, signal)
    pl.semaphore_wait(barrier, 2 + len(near))

    def tell(step, peers):
        for _, where in peers:
            pl.semaphore_signal(in_sem.at[step], inc=1, device_id=where, device_id_type=MESH)

    def heard(step, peers):
        pl.semaphore_wait(in_sem.at[step], len(peers))

    steps = [near]
    if n_y > 4 or n_case > 4:
        steps.append([m_peer((0, 2)), m_peer((0, n_y - 2)), z_peer(2), z_peer(n_case - 2)])
    steps.append([m_peer((dx, 0)) for dx in range(1, n_x)])
    tell(0, steps[0])

    def remote(src, dst, send_sem, recv_sem, where):
        return pltpu.make_async_remote_copy(
            src_ref=src,
            dst_ref=dst,
            send_sem=send_sem,
            recv_sem=recv_sem,
            device_id=where,
            device_id_type=MESH,
        )

    halves = (1 - core, core)

    def rows_of(p, first=0):
        return pl.ds(pl.multiple_of(first + p * PATCH, PATCH), PATCH)

    def side_rows(p):
        return pl.ds(pl.multiple_of(p * (HALF + LEN), HALF), HALF)

    def to_side(i, src, first_row, win, at):
        where = to_sib if i == 0 else {"pt": outer, "case": case}
        p = halves[i]
        copy = remote(
            src.at[rows_of(p, first_row)],
            win.at[side_rows(1 - p)],
            ex_send.at[at + i],
            ex_recv.at[at + i],
            where,
        )
        copy.start()
        return copy

    ex_p = [to_side(i, points, 0, point_win, 0) for i in (1, 0)][::-1]
    ex_c = [to_side(i, cotangent, 0, cot_win, 2) for i in (1, 0)][::-1]
    ex_out = [None, None]
    ex_grad = [None, None]

    own = pl.ds(HALF, LEN)
    offset = pt * LEN - HALF

    for load in loads[:3]:
        load.wait()
    hots = []
    for i, p in enumerate(halves):
        row = from_s[:, rows_of(p)] - offset
        hot = one_hot(row, HALF, LEN)
        hilbert_p[i] = nn(hot, point_win[own, :])
        hilbert_c[i] = nn(hot, cot_win[own, :])
        hots.append(one_hot(row, p * (HALF + LEN), HALF))
    for load in loads[3:]:
        load.wait()
    heard(0, steps[0])
    tell(1, steps[1])

    def heard_rings():
        if len(steps) == 3:
            heard(1, steps[1])
            tell(2, steps[2])

    gain = gain_s[...]
    lane_head = lax.broadcasted_iota(jnp.int32, (1, 128), 1) // HEAD
    masks = [jnp.where(lane_head == h, 1.0, 0.0).astype(BF16) for h in range(4)]

    def project(i):
        p = halves[i]
        ex_p[i].wait_recv()
        features = hilbert_p[i] + nn(hots[i], point_win[side_rows(p), :])
        hilbert_p[i] = features
        centered = features - jnp.mean(features, axis=-1, keepdims=True)
        inverse = lax.rsqrt(jnp.mean(centered * centered, axis=-1, keepdims=True) + epsilon)
        standard = centered * inverse
        standard_s[i] = standard
        inverse_s[i] = jnp.broadcast_to(inverse, (PATCH, 128))
        normed = (standard * gain + bias_s[...]).astype(BF16)
        normed_t_s[i] = jnp.transpose(normed)
        proj_s[i] = (nn(normed, w_qkv[...]) + b_qkv_s[...]).astype(BF16)
        ex_c[i].wait_recv()
        cot = hilbert_c[i] + nn(hots[i], cot_win[side_rows(p), :])
        hilbert_c[i] = cot
        d_att_s[i] = nt(cot.astype(BF16), w_out[...]).astype(BF16)

    def first_pass(i):
        for block in range(2):
            b0 = block * 128
            q = proj_s[i, :, pl.ds(b0, 128)]
            k = proj_s[i, :, pl.ds(256 + b0, 128)]
            v_t = jnp.transpose(proj_s[i, :, pl.ds(512 + b0, 128)])
            da = d_att_s[i, :, pl.ds(b0, 128)]
            d_v = None
            for h in range(4):
                mask = masks[h]
                exponent = jnp.exp2(nt(k * mask, q) * EXP2_SCALE)
                total = jnp.sum(exponent, axis=0, keepdims=True)
                prob = exponent * (1.0 / total)
                prob_s[block * 4 + h] = prob
                prob_low = prob.astype(BF16)
                att_t = nn(v_t[h * HEAD : (h + 1) * HEAD], prob_low)
                attended_t_s[i, pl.ds(b0 + h * HEAD, HEAD), :] = att_t.astype(BF16)
                d_v_h = nn(prob_low, da * mask)
                d_v = d_v_h if d_v is None else d_v + d_v_h
            d_proj_s[i, :, pl.ds(512 + b0, 128)] = d_v.astype(BF16)

    def block_output(i):
        attended = jnp.transpose(attended_t_s[i])
        branch = nn(attended, w_out[...]) + b_out_s[...]
        out_win[rows_of(halves[i], HALF), :] = (hilbert_p[i] + branch).astype(BF16)
        if i == 0:
            ex_out[i] = to_side(i, out_win, HALF, out_win, 4)

    def second_pass(i, block):
        b0 = block * 128
        q = proj_s[i, :, pl.ds(b0, 128)]
        k_t = jnp.transpose(proj_s[i, :, pl.ds(256 + b0, 128)])
        v = proj_s[i, :, pl.ds(512 + b0, 128)]
        da = d_att_s[i, :, pl.ds(b0, 128)]
        d_q_t = []
        d_k = None
        for h in range(4):
            mask = masks[h]
            prob = prob_s[block * 4 + h]
            d_prob = nt(v * mask, da)
            row_sum = jnp.sum(prob * d_prob, axis=0, keepdims=True)
            d_s = (prob * (d_prob - row_sum) * SCALE).astype(BF16)
            d_k_h = nn(d_s, q * mask)
            d_k = d_k_h if d_k is None else d_k + d_k_h
            d_q_t.append(nn(k_t[h * HEAD : (h + 1) * HEAD], d_s))
        d_q = jnp.transpose(jnp.concatenate(d_q_t, axis=0))
        d_proj_s[i, :, pl.ds(b0, 128)] = d_q.astype(BF16)
        d_proj_s[i, :, pl.ds(256 + b0, 128)] = d_k.astype(BF16)

    def add(ref, index, value, i):
        ref[index] = value if i == 0 else ref[index] + value

    def forward_terms(i):
        d_v = d_proj_s[i, :, pl.ds(512, 256)]
        add(acc1, 0, to_tiles(nn(normed_t_s[i], d_v)), i)
        add(acc1, 1, to_tiles(nn(attended_t_s[i], hilbert_c[i].astype(BF16))), i)

    def backward_terms(i):
        d_proj = d_proj_s[i]
        d_normed = nt(d_proj, w_qkv[...])
        d_normed_s[...] = d_normed
        sums = (
            (0, jnp.sum(d_proj.astype(F32), axis=0, keepdims=True)),
            (8, jnp.sum(hilbert_c[i], axis=0, keepdims=True)),
            (10, jnp.sum(d_normed * standard_s[i], axis=0, keepdims=True)),
            (12, jnp.sum(d_normed, axis=0, keepdims=True)),
        )
        if i == 0:
            vector_s[...] = jnp.zeros((16, 128), F32)
        for row, value in sums:
            for part in range(value.shape[1] // 128):
                add(
                    vector_s,
                    slice(row + part, row + part + 1),
                    value[:, part * 128 : part * 128 + 128],
                    i,
                )
        add(acc2, 0, to_tiles(nn(normed_t_s[i], d_proj[:, :256])), i)
        add(acc2, 1, to_tiles(nn(normed_t_s[i], d_proj[:, 256:512])), i)

    def norm_backward(i):
        d_normed = d_normed_s[...]
        standard = standard_s[i]
        scaled = d_normed * gain
        inverse = inverse_s[i]
        inverse = jnp.concatenate([inverse, inverse], axis=1)
        d_input = inverse * (
            scaled
            - jnp.mean(scaled, axis=-1, keepdims=True)
            - standard * jnp.mean(scaled * standard, axis=-1, keepdims=True)
        )
        grad_win[rows_of(halves[i], HALF), :] = (hilbert_c[i] + d_input).astype(BF16)
        if i == 0:
            ex_grad[i] = to_side(i, grad_win, HALF, grad_win, 6)

    chunks = (
        (acc1, core_send1, core_recv1, m_send1, m_recv1, z_recv1, sums1),
        (acc2, core_send2, core_recv2, m_send2, m_recv2, z_recv2, sums2),
    )
    pers = (TILES // (n_x * n_y), TILES // (n_x * n_case))

    def sem(chunk, stage):
        return ar_send.at[chunk * 5 + stage], ar_recv.at[chunk * 5 + stage]

    def wait_total(ref, semaphore):
        pltpu.make_async_copy(ref, ref, semaphore).wait()

    def high_low(value):
        high = value.astype(BF16)
        low = (value - high.astype(F32)).astype(BF16)
        return jnp.concatenate([high, low], axis=0)

    def joined(tile):
        tile = tile.astype(F32)
        return tile[:8] + tile[8:]

    def core_start(chunk):
        acc, send, recv = chunks[chunk][:3]
        send[pl.ds(0, TILES)] = acc[1 - core].astype(BF16)
        if chunk:
            theirs = pl.multiple_of((1 - core) * 8, 8)
            send[TILES] = high_low(vector_s[pl.ds(theirs, 8), :])
        copy = remote(send, recv, *sem(chunk, 0), to_sib)
        copy.start()
        return copy

    def m_start(chunk, copy):
        acc, _, recv0, send, recv = chunks[chunk][:5]
        at, peers = planes[chunk]
        if chunk == 0:
            copy.wait()
        half = (acc[core] + recv0[pl.ds(0, TILES)].astype(F32)).astype(BF16)
        send[...] = half.reshape(len(peers) + 1, pers[chunk], 16, 128)
        recv[pl.ds(at, 1)] = send[pl.ds(at, 1)]
        s, r = sem(chunk, 1)
        for to, where in peers:
            remote(send.at[to], recv.at[at], s, r, where).start()

    def z_start(chunk):
        recv0, recv = chunks[chunk][4:6]
        at, peers = lines[chunk]
        wait_total(recv0.at[pl.ds(0, len(planes[chunk][1]))], sem(chunk, 1)[1])
        recv[at] = jnp.sum(recv0[...].astype(F32), axis=0).astype(BF16)
        s, r = sem(chunk, 2)
        slot = recv.at[at]
        for _, where in peers:
            remote(slot, slot, s, r, where).start()

    def m_back(chunk):
        recv0, result = chunks[chunk][5:7]
        at, peers = planes[chunk]
        wait_total(recv0.at[pl.ds(0, len(lines[chunk][1]))], sem(chunk, 2)[1])
        rows = pl.ds(at * pers[chunk], pers[chunk])
        result[core, rows] = jnp.sum(recv0[...].astype(F32), axis=0).astype(BF16)
        s, r = sem(chunk, 3)
        slot = result.at[core, rows]
        for _, where in peers:
            remote(slot, slot, s, r, where).start()

    def core_back(chunk):
        result = chunks[chunk][6]
        wait_total(result.at[core, pl.ds(0, len(planes[chunk][1]) * pers[chunk])], sem(chunk, 3)[1])
        slot = result.at[core, pl.ds(0, TILES)]
        copy = remote(slot, slot, *sem(chunk, 4), to_sib)
        copy.start()
        return copy

    def vec_line_start(copy):
        copy.wait()
        at, peers = lines[1]
        mine = pl.multiple_of(core * 8, 8)
        vec_z[at] = high_low(vector_s[pl.ds(mine, 8), :] + joined(core_recv2[TILES]))
        slot = vec_z.at[at]
        for _, where in peers:
            remote(slot, slot, ar_send.at[10], ar_recv.at[10], where).start()

    def vec_plane_start():
        at, peers = planes[1]
        count = len(lines[1][1])
        wait_total(vec_z.at[pl.ds(0, count)], ar_recv.at[10])
        total = joined(vec_z[0])
        for i in range(1, count + 1):
            total = total + joined(vec_z[i])
        vec_m[at] = high_low(total)
        slot = vec_m.at[at]
        for _, where in peers:
            remote(slot, slot, ar_send.at[11], ar_recv.at[11], where).start()

    def vec_back():
        wait_total(vec_m.at[pl.ds(0, len(planes[1][1]))], ar_recv.at[11])
        total = jnp.sum(vec_m[...].astype(F32), axis=0)
        sums2[core, TILES] = high_low(total[:8] + total[8:])
        slot = sums2.at[core, TILES]
        copy = remote(slot, slot, ar_send.at[12], ar_recv.at[12], to_sib)
        copy.start()
        return copy

    def finish(chunk, copy):
        send1, _, recv2, result = chunks[chunk][3:7]
        count = len(planes[chunk][1])
        wait_total(send1.at[pl.ds(0, count)], sem(chunk, 1)[0])
        wait_total(recv2.at[pl.ds(0, len(lines[chunk][1]))], sem(chunk, 2)[0])
        wait_total(result.at[core, pl.ds(0, count * pers[chunk])], sem(chunk, 3)[0])
        copy.wait()

    project(0)
    first_pass(0)
    block_output(0)
    heard_rings()
    second_pass(0, 0)
    second_pass(0, 1)
    forward_terms(0)
    backward_terms(0)
    norm_backward(0)
    project(1)
    heard(len(steps) - 1, steps[-1])
    first_pass(1)
    forward_terms(1)
    core_copy1 = core_start(0)
    block_output(1)
    second_pass(1, 0)
    m_start(0, core_copy1)
    second_pass(1, 1)
    backward_terms(1)
    core_copy2 = core_start(1)
    norm_backward(1)

    def to_z_order(pair, win, stage, result, at):
        for copy in pair:
            copy.wait_recv()
        for p in range(2):
            row = to_s[:, p * PATCH : (p + 1) * PATCH] - offset
            hot = one_hot(row, p * HALF, HALF + LEN)
            at_p = pl.ds(p * PATCH, PATCH)
            stage[at_p, :] = nn(hot, win[pl.ds(p * HALF, HALF + LEN), :]).astype(BF16)
        store = pltpu.make_async_copy(stage, result, local_sem.at[at])
        store.start()
        return store

    vec_line_start(core_copy2)
    m_start(1, None)
    ex_out[1] = to_side(1, out_win, HALF, out_win, 4)
    ex_grad[1] = to_side(1, grad_win, HALF, grad_win, 6)
    z_start(0)
    vec_plane_start()
    z_start(1)
    store_out = to_z_order(ex_out, out_win, out_stage, output, 10)
    m_back(0)
    m_back(1)
    store_grad = to_z_order(ex_grad, grad_win, grad_stage, grad_points, 11)
    last1 = core_back(0)
    vec_last = vec_back()
    last2 = core_back(1)
    finish(0, last1)
    wait_total(vec_z.at[pl.ds(0, len(lines[1][1]))], ar_send.at[10])
    wait_total(vec_m.at[pl.ds(0, len(planes[1][1]))], ar_send.at[11])
    for pair in (ex_p, ex_c, ex_out, ex_grad):
        for copy in pair:
            copy.wait_send()
    store_out.wait()
    store_grad.wait()
    vec_last.wait()
    finish(1, last2)


def results_kernel(
    factor,
    output_in,
    grad_in,
    sums1_in,
    sums2_in,
    output,
    grad_points,
    grad_w_qkv,
    grad_b_qkv,
    grad_w_out,
    grad_b_out,
    grad_gain,
    grad_bias,
    output_s,
    grad_s,
    sums1,
    sums2,
    w_qkv_s,
    w_out_s,
    vec_s,
    in_sems,
    out_sems,
):
    loads = [(sums1_in, sums1), (sums2_in, sums2), (output_in, output_s), (grad_in, grad_s)]
    loads = [pltpu.make_async_copy(a, b, in_sems.at[i]) for i, (a, b) in enumerate(loads)]
    for load in loads:
        load.start()
    stores = []

    def store(a, b):
        stores.append(pltpu.make_async_copy(a, b, out_sems.at[len(stores)]))
        stores[-1].start()

    def block(sums, c, half):
        return sums[c, pl.ds(half * 16, 16)].reshape(256, 128).astype(F32) * factor

    def weight(sums, c, stage, first, result):
        for half in range(2):
            stage[:, pl.ds(first + half * 128, 128)] = block(sums, c, half)
        columns = pl.ds(first, D)
        store(stage.at[:, columns], result.at[:, columns])

    loads[0].wait()
    weight(sums1, 0, w_qkv_s, 512, grad_w_qkv)
    weight(sums1, 1, w_out_s, 0, grad_w_out)
    loads[1].wait()
    weight(sums2, 0, w_qkv_s, 0, grad_w_qkv)
    weight(sums2, 1, w_qkv_s, 256, grad_w_qkv)
    vectors = []
    for c in range(2):
        tile = sums2[c, TILES].astype(F32)
        vectors.append((tile[:8] + tile[8:]) * factor)
    for part in range(6):
        vec_s[0:1, part * 128 : part * 128 + 128] = vectors[0][part : part + 1]
        row = 1 + part // 2
        vec_s[row : row + 1, (part % 2) * 128 : (part % 2) * 128 + 128] = vectors[1][part : part + 1]
    store(vec_s.at[0], grad_b_qkv)
    store(vec_s.at[1, pl.ds(0, D)], grad_b_out)
    store(vec_s.at[2, pl.ds(0, D)], grad_gain)
    store(vec_s.at[3, pl.ds(0, D)], grad_bias)
    loads[2].wait()
    store(output_s, output)
    loads[3].wait()
    store(grad_s, grad_points)
    for copy in stores:
        copy.wait()


def on_device(n_pt, n_case, n_x, n_y, points, cotangent, to_hilbert, from_hilbert, *params):
    plane1, plane2 = n_x * n_y, n_x * n_case
    per1, per2 = TILES // plane1, TILES // plane2
    vmem = pl.BlockSpec(memory_space=pltpu.VMEM)
    hbm = pl.BlockSpec(memory_space=pl.ANY)
    shape = jax.ShapeDtypeStruct
    rows = shape((LEN, D), BF16)

    def tiles(*lead):
        return pltpu.VMEM((*lead, 16, 128), BF16)

    output, grad_points, sums1, sums2 = pl.pallas_call(
        functools.partial(kernel, n_pt, n_case, n_x, n_y),
        out_shape=(
            rows,
            rows,
            shape((2, TILES, 16, 128), BF16),
            shape((2, TILES + 1, 16, 128), BF16),
        ),
        in_specs=[hbm] * 10,
        out_specs=(hbm, hbm, vmem, vmem),
        scratch_shapes=[
            pltpu.VMEM((1, LEN), jnp.int32),
            pltpu.VMEM((1, LEN), jnp.int32),
            pltpu.VMEM((1, D), F32),
            pltpu.VMEM((1, D), F32),
            pltpu.VMEM((1, 3 * D), F32),
            pltpu.VMEM((1, D), F32),
            pltpu.VMEM((D, 3 * D), BF16),
            pltpu.VMEM((D, D), BF16),
            pltpu.VMEM((WIN, D), BF16),
            pltpu.VMEM((WIN, D), BF16),
            pltpu.VMEM((WIN, D), BF16),
            pltpu.VMEM((WIN, D), BF16),
            pltpu.VMEM((2, PATCH, D), F32),
            pltpu.VMEM((2, PATCH, D), F32),
            pltpu.VMEM((2, PATCH, D), F32),
            pltpu.VMEM((2, PATCH, 128), F32),
            pltpu.VMEM((2, D, PATCH), BF16),
            pltpu.VMEM((2, PATCH, 3 * D), BF16),
            pltpu.VMEM((2, PATCH, D), BF16),
            pltpu.VMEM((8, PATCH, PATCH), F32),
            pltpu.VMEM((2, D, PATCH), BF16),
            pltpu.VMEM((2, PATCH, 3 * D), BF16),
            pltpu.VMEM((PATCH, D), F32),
            pltpu.VMEM((16, 128), F32),
            pltpu.VMEM((2, TILES, 16, 128), F32),
            pltpu.VMEM((2, TILES, 16, 128), F32),
            tiles(TILES),
            tiles(TILES + 1),
            tiles(TILES),
            tiles(TILES + 1),
            tiles(plane1, per1),
            tiles(plane2, per2),
            tiles(plane1, per1),
            tiles(plane2, per2),
            tiles(n_case, per1),
            tiles(n_y, per2),
            tiles(n_y),
            tiles(plane2),
            pltpu.VMEM((LEN, D), BF16),
            pltpu.VMEM((LEN, D), BF16),
            pltpu.SemaphoreType.DMA((12,)),
            pltpu.SemaphoreType.DMA((8,)),
            pltpu.SemaphoreType.DMA((8,)),
            pltpu.SemaphoreType.DMA((14,)),
            pltpu.SemaphoreType.DMA((14,)),
            pltpu.SemaphoreType.REGULAR((3,)),
        ],
        compiler_params=pltpu.CompilerParams(
            collective_id=0, has_side_effects=True, vmem_limit_bytes=VMEM_LIMIT
        ),
    )(points[0], cotangent[0], to_hilbert, from_hilbert, *params)
    factor = 1.0 / math.sqrt(n_pt * n_case * LEN)
    result = pl.pallas_call(
        functools.partial(results_kernel, factor),
        out_shape=(
            rows,
            rows,
            shape((D, 3 * D), F32),
            shape((3 * D,), F32),
            shape((D, D), F32),
            shape((D,), F32),
            shape((D,), F32),
            shape((D,), F32),
        ),
        in_specs=[hbm] * 4,
        out_specs=(hbm,) * 8,
        scratch_shapes=[
            pltpu.VMEM((LEN, D), BF16),
            pltpu.VMEM((LEN, D), BF16),
            tiles(2, TILES),
            tiles(2, TILES + 1),
            pltpu.VMEM((D, 3 * D), F32),
            pltpu.VMEM((D, D), F32),
            pltpu.VMEM((4, 3 * D), F32),
            pltpu.SemaphoreType.DMA((4,)),
            pltpu.SemaphoreType.DMA((10,)),
        ],
        compiler_params=pltpu.CompilerParams(vmem_limit_bytes=VMEM_LIMIT),
    )(output, grad_points, sums1, sums2)
    return (result[0][None], result[1][None], *result[2:])


def solution(mesh):
    n_pt, n_case = mesh.shape["pt"], mesh.shape["case"]
    members = n_pt // 2
    n_y = 8 if members >= 32 else 2
    rows = P("case", "pt", None)
    index = P("case", "pt")
    return jax.shard_map(
        functools.partial(on_device, n_pt, n_case, members // n_y, n_y),
        mesh=mesh,
        in_specs=(rows, rows, index, index) + (P(),) * 6,
        out_specs=(rows, rows) + (P(),) * 6,
        check_vma=False,
    )
```

```python
import functools
import math

import jax
import jax.numpy as jnp
from jax import lax
from jax.experimental import pallas as pl
from jax.experimental.pallas import tpu as pltpu
from jax.sharding import PartitionSpec as P

D = 256
HEADS = 8
HEAD = 32
PATCH = 256
LEN = 512
HALF = 256
WIN = 1024
TILES = 32
epsilon = 1e-05
VMEM_LIMIT = 60 * 1024 * 1024
SCALE = 1.0 / math.sqrt(HEAD)
EXP2_SCALE = SCALE * math.log2(math.e)

MESH = pl.DeviceIdType.MESH
F32 = jnp.float32
BF16 = jnp.bfloat16


def nn(a, b):
    return lax.dot_general(a, b, (((1,), (0,)), ((), ())), preferred_element_type=F32)


def nt(a, b):
    return lax.dot_general(a, b, (((1,), (1,)), ((), ())), preferred_element_type=F32)


def one_hot(index_row, low, width):
    columns = [
        jnp.transpose(jnp.broadcast_to(index_row[:, a : a + 128], (128, 128))) for a in (0, 128)
    ]
    column = jnp.concatenate(columns, axis=0) - low
    lane = lax.broadcasted_iota(jnp.int32, (256, 128), 1)
    return jnp.concatenate(
        [jnp.where(column == lane + b, 1.0, 0.0).astype(BF16) for b in range(0, width, 128)],
        axis=1,
    )


def ring_order(n_x, n_y):
    places = [(x, y) for x in range(n_x) for y in range(n_y) if x or y]
    return sorted(places, key=lambda p: -(min(p[0], n_x - p[0]) + min(p[1], n_y - p[1])))


def to_tiles(block):
    return jnp.concatenate([block[:, a : a + 128].reshape(16, 16, 128) for a in (0, 128)], axis=0)


def kernel(
    n_pt,
    n_case,
    n_x,
    n_y,
    points,
    cotangent,
    to_hilbert,
    from_hilbert,
    ln_gain,
    ln_bias,
    w_qkv_in,
    b_qkv,
    w_out_in,
    b_out,
    output,
    grad_points,
    sums1,
    sums2,
    to_s,
    from_s,
    gain_s,
    bias_s,
    b_qkv_s,
    b_out_s,
    w_qkv,
    w_out,
    point_win,
    cot_win,
    out_win,
    grad_win,
    hilbert_p,
    hilbert_c,
    standard_s,
    inverse_s,
    normed_t_s,
    proj_s,
    d_att_s,
    prob_s,
    attended_t_s,
    d_proj_s,
    d_normed_s,
    vector_s,
    acc1,
    acc2,
    core_send1,
    core_send2,
    core_recv1,
    core_recv2,
    m_send1,
    m_send2,
    m_recv1,
    m_recv2,
    z_recv1,
    z_recv2,
    vec_z,
    vec_m,
    own_sum1,
    own_sum2,
    out_stage,
    grad_stage,
    local_sem,
    ex_send,
    ex_recv,
    ar_send,
    ar_recv,
    in_sem,
):
    pt = lax.axis_index("pt")
    case = lax.axis_index("case")
    core = lax.rem(pt, 2)
    member = lax.div(pt, 2)
    sibling = pt + 1 - 2 * core
    outer = lax.rem(pt + n_pt - 1 + 2 * core, n_pt)

    x_at = lax.div(member, n_y)
    y_at = lax.rem(member, n_y)

    def m_peer(place):
        to = lax.rem(x_at + place[0], n_x) * n_y + lax.rem(y_at + place[1], n_y)
        return to, {"pt": to * 2 + core, "case": case}

    def z_peer(r):
        to = lax.rem(case + r, n_case)
        return to, {"pt": pt, "case": to}

    def xz_peer(place):
        x_to = lax.rem(x_at + place[0], n_x)
        z_to = lax.rem(case + place[1], n_case)
        return x_to * n_case + z_to, {"pt": (x_to * n_y + y_at) * 2 + core, "case": z_to}

    def y_peer(r):
        to = lax.rem(y_at + r, n_y)
        return to, {"pt": (x_at * n_y + to) * 2 + core, "case": case}

    xy_peers = [m_peer(place) for place in ring_order(n_x, n_y)]
    z_peers = [z_peer(r) for _, r in ring_order(1, n_case)]
    xz_peers = [xz_peer(place) for place in ring_order(n_x, n_case)]
    y_peers = [y_peer(r) for _, r in ring_order(1, n_y)]
    planes = ((member, xy_peers), (x_at * n_case + case, xz_peers))
    lines = ((case, z_peers), (y_at, y_peers))

    def for_peers(peers, body):
        for peer in peers:
            body(*peer)

    barrier = pltpu.get_barrier_semaphore()

    def signal(_, where):
        pl.semaphore_signal(barrier, inc=1, device_id=where, device_id_type=MESH)

    to_sib = {"pt": sibling, "case": case}
    signal(None, {"pt": outer, "case": case})
    signal(None, to_sib)
    near = [m_peer((0, 1)), m_peer((0, n_y - 1)), m_peer((1, 0)), m_peer((n_x - 1, 0))]
    near += [z_peer(1), z_peer(n_case - 1)]
    for_peers(near, signal)
    loads = [
        (points, point_win.at[pl.ds(HALF, LEN)]),
        (cotangent, cot_win.at[pl.ds(HALF, LEN)]),
        (from_hilbert, from_s),
        (ln_gain, gain_s.at[0]),
        (ln_bias, bias_s.at[0]),
        (w_qkv_in, w_qkv),
        (b_qkv, b_qkv_s.at[0]),
        (w_out_in, w_out),
        (b_out, b_out_s.at[0]),
        (to_hilbert, to_s),
    ]
    loads = [pltpu.make_async_copy(a, b, local_sem.at[i]) for i, (a, b) in enumerate(loads)]
    for load in loads:
        load.start()
    pl.semaphore_wait(barrier, 2 + len(near))

    def tell(step, peers):
        for _, where in peers:
            pl.semaphore_signal(in_sem.at[step], inc=1, device_id=where, device_id_type=MESH)

    def heard(step, peers):
        pl.semaphore_wait(in_sem.at[step], len(peers))

    steps = [near]
    if n_y > 4 or n_case > 4:
        steps.append([m_peer((0, 2)), m_peer((0, n_y - 2)), z_peer(2), z_peer(n_case - 2)])
    steps.append([m_peer((dx, 0)) for dx in range(1, n_x)])
    tell(0, steps[0])

    def remote(src, dst, send_sem, recv_sem, where):
        return pltpu.make_async_remote_copy(
            src_ref=src,
            dst_ref=dst,
            send_sem=send_sem,
            recv_sem=recv_sem,
            device_id=where,
            device_id_type=MESH,
        )

    halves = (1 - core, core)

    def rows_of(p, first=0):
        return pl.ds(pl.multiple_of(first + p * PATCH, PATCH), PATCH)

    def side_rows(p):
        return pl.ds(pl.multiple_of(p * (HALF + LEN), HALF), HALF)

    def to_side(i, src, first_row, win, at):
        where = to_sib if i == 0 else {"pt": outer, "case": case}
        p = halves[i]
        copy = remote(
            src.at[rows_of(p, first_row)],
            win.at[side_rows(1 - p)],
            ex_send.at[at + i],
            ex_recv.at[at + i],
            where,
        )
        copy.start()
        return copy

    ex_p = [to_side(i, points, 0, point_win, 0) for i in (1, 0)][::-1]
    ex_c = [to_side(i, cotangent, 0, cot_win, 2) for i in (1, 0)][::-1]
    ex_out = [None, None]
    ex_grad = [None, None]

    own = pl.ds(HALF, LEN)
    offset = pt * LEN - HALF

    for load in loads[:3]:
        load.wait()
    hots = []
    for i, p in enumerate(halves):
        row = from_s[:, rows_of(p)] - offset
        hot = one_hot(row, HALF, LEN)
        hilbert_p[i] = nn(hot, point_win[own, :])
        hilbert_c[i] = nn(hot, cot_win[own, :])
        hots.append(one_hot(row, p * (HALF + LEN), HALF))
    for load in loads[3:]:
        load.wait()
    heard(0, steps[0])
    tell(1, steps[1])

    def heard_rings():
        if len(steps) == 3:
            heard(1, steps[1])
            tell(2, steps[2])

    gain = gain_s[...]
    lane_head = lax.broadcasted_iota(jnp.int32, (1, 128), 1) // HEAD
    masks = [jnp.where(lane_head == h, 1.0, 0.0).astype(BF16) for h in range(4)]

    def project(i):
        p = halves[i]
        ex_p[i].wait_recv()
        features = hilbert_p[i] + nn(hots[i], point_win[side_rows(p), :])
        hilbert_p[i] = features
        centered = features - jnp.mean(features, axis=-1, keepdims=True)
        inverse = lax.rsqrt(jnp.mean(centered * centered, axis=-1, keepdims=True) + epsilon)
        standard = centered * inverse
        standard_s[i] = standard
        inverse_s[i] = jnp.broadcast_to(inverse, (PATCH, 128))
        normed = (standard * gain + bias_s[...]).astype(BF16)
        normed_t_s[i] = jnp.transpose(normed)
        proj_s[i] = (nn(normed, w_qkv[...]) + b_qkv_s[...]).astype(BF16)

    def project_cotangent(i):
        p = halves[i]
        ex_c[i].wait_recv()
        cot = hilbert_c[i] + nn(hots[i], cot_win[side_rows(p), :])
        hilbert_c[i] = cot
        d_att_s[i] = nt(cot.astype(BF16), w_out[...]).astype(BF16)

    def first_pass(i):
        for block in range(2):
            b0 = block * 128
            q = proj_s[i, :, pl.ds(b0, 128)]
            k = proj_s[i, :, pl.ds(256 + b0, 128)]
            v_t = jnp.transpose(proj_s[i, :, pl.ds(512 + b0, 128)])
            for h in range(4):
                exponent = jnp.exp2(nt(k * masks[h], q) * EXP2_SCALE)
                total = jnp.sum(exponent, axis=0, keepdims=True)
                prob = exponent * (1.0 / total)
                prob_s[block * 4 + h] = prob
                prob_low = prob.astype(BF16)
                att_t = nn(v_t[h * HEAD : (h + 1) * HEAD], prob_low)
                attended_t_s[i, pl.ds(b0 + h * HEAD, HEAD), :] = att_t.astype(BF16)

    def block_output(i):
        attended = jnp.transpose(attended_t_s[i])
        branch = nn(attended, w_out[...]) + b_out_s[...]
        out_win[rows_of(halves[i], HALF), :] = (hilbert_p[i] + branch).astype(BF16)
        if i == 0:
            ex_out[i] = to_side(i, out_win, HALF, out_win, 4)

    def second_pass(i, block):
        b0 = block * 128
        q = proj_s[i, :, pl.ds(b0, 128)]
        k_t = jnp.transpose(proj_s[i, :, pl.ds(256 + b0, 128)])
        v = proj_s[i, :, pl.ds(512 + b0, 128)]
        da = d_att_s[i, :, pl.ds(b0, 128)]
        d_q_t = []
        d_k = None
        d_v = None
        for h in range(4):
            mask = masks[h]
            prob = prob_s[block * 4 + h]
            d_v_h = nn(prob.astype(BF16), da * mask)
            d_v = d_v_h if d_v is None else d_v + d_v_h
            d_prob = nt(v * mask, da)
            row_sum = jnp.sum(prob * d_prob, axis=0, keepdims=True)
            d_s = (prob * (d_prob - row_sum) * SCALE).astype(BF16)
            d_k_h = nn(d_s, q * mask)
            d_k = d_k_h if d_k is None else d_k + d_k_h
            d_q_t.append(nn(k_t[h * HEAD : (h + 1) * HEAD], d_s))
        d_q = jnp.transpose(jnp.concatenate(d_q_t, axis=0))
        d_proj_s[i, :, pl.ds(b0, 128)] = d_q.astype(BF16)
        d_proj_s[i, :, pl.ds(256 + b0, 128)] = d_k.astype(BF16)
        d_proj_s[i, :, pl.ds(512 + b0, 128)] = d_v.astype(BF16)

    def add(ref, index, value, i):
        ref[index] = value if i == 0 else ref[index] + value

    def forward_terms(i):
        d_v = d_proj_s[i, :, pl.ds(512, 256)]
        add(acc1, 0, to_tiles(nn(normed_t_s[i], d_v)), i)
        add(acc1, 1, to_tiles(nn(attended_t_s[i], hilbert_c[i].astype(BF16))), i)

    def backward_terms(i):
        d_proj = d_proj_s[i]
        d_normed = nt(d_proj, w_qkv[...])
        d_normed_s[...] = d_normed
        sums = (
            (0, jnp.sum(d_proj.astype(F32), axis=0, keepdims=True)),
            (8, jnp.sum(hilbert_c[i], axis=0, keepdims=True)),
            (10, jnp.sum(d_normed * standard_s[i], axis=0, keepdims=True)),
            (12, jnp.sum(d_normed, axis=0, keepdims=True)),
        )
        if i == 0:
            vector_s[...] = jnp.zeros((16, 128), F32)
        for row, value in sums:
            for part in range(value.shape[1] // 128):
                add(
                    vector_s,
                    slice(row + part, row + part + 1),
                    value[:, part * 128 : part * 128 + 128],
                    i,
                )
        add(acc2, 0, to_tiles(nn(normed_t_s[i], d_proj[:, :256])), i)
        add(acc2, 1, to_tiles(nn(normed_t_s[i], d_proj[:, 256:512])), i)

    def norm_backward(i):
        d_normed = d_normed_s[...]
        standard = standard_s[i]
        scaled = d_normed * gain
        inverse = inverse_s[i]
        inverse = jnp.concatenate([inverse, inverse], axis=1)
        d_input = inverse * (
            scaled
            - jnp.mean(scaled, axis=-1, keepdims=True)
            - standard * jnp.mean(scaled * standard, axis=-1, keepdims=True)
        )
        grad_win[rows_of(halves[i], HALF), :] = (hilbert_c[i] + d_input).astype(BF16)
        if i == 0:
            ex_grad[i] = to_side(i, grad_win, HALF, grad_win, 6)

    chunks = (
        (acc1, core_send1, core_recv1, m_send1, m_recv1, z_recv1, own_sum1),
        (acc2, core_send2, core_recv2, m_send2, m_recv2, z_recv2, own_sum2),
    )
    pers = (TILES // (n_x * n_y), TILES // (n_x * n_case))

    def sem(chunk, stage):
        return ar_send.at[chunk * 5 + stage], ar_recv.at[chunk * 5 + stage]

    def wait_total(ref, semaphore):
        pltpu.make_async_copy(ref, ref, semaphore).wait()

    def high_low(value):
        high = value.astype(BF16)
        low = (value - high.astype(F32)).astype(BF16)
        return jnp.concatenate([high, low], axis=0)

    def joined(tile):
        tile = tile.astype(F32)
        return tile[:8] + tile[8:]

    def core_start(chunk):
        acc, send, recv = chunks[chunk][:3]
        send[pl.ds(0, TILES)] = acc[1 - core].astype(BF16)
        if chunk:
            theirs = pl.multiple_of((1 - core) * 8, 8)
            send[TILES] = high_low(vector_s[pl.ds(theirs, 8), :])
        copy = remote(send, recv, *sem(chunk, 0), to_sib)
        copy.start()
        return copy

    def m_start(chunk, copy):
        acc, _, recv0, send, recv = chunks[chunk][:5]
        at, peers = planes[chunk]
        copy.wait()
        half = (acc[core] + recv0[pl.ds(0, TILES)].astype(F32)).astype(BF16)
        send[...] = half.reshape(len(peers) + 1, pers[chunk], 16, 128)
        recv[pl.ds(at, 1)] = send[pl.ds(at, 1)]
        s, r = sem(chunk, 1)
        for to, where in peers:
            remote(send.at[to], recv.at[at], s, r, where).start()

    def z_start(chunk):
        recv0, recv = chunks[chunk][4:6]
        at, peers = lines[chunk]
        wait_total(recv0.at[pl.ds(0, len(planes[chunk][1]))], sem(chunk, 1)[1])
        recv[at] = jnp.sum(recv0[...].astype(F32), axis=0).astype(BF16)
        s, r = sem(chunk, 2)
        slot = recv.at[at]
        for _, where in peers:
            remote(slot, slot, s, r, where).start()

    def m_back(chunk):
        recv0, result = chunks[chunk][5:7]
        at, peers = planes[chunk]
        wait_total(recv0.at[pl.ds(0, len(lines[chunk][1]))], sem(chunk, 2)[1])
        rows = pl.ds(at * pers[chunk], pers[chunk])
        result[rows] = jnp.sum(recv0[...].astype(F32), axis=0).astype(BF16)
        s, r = sem(chunk, 3)
        slot = result.at[rows]
        for _, where in peers:
            remote(slot, slot, s, r, where).start()

    def core_back(chunk):
        result = chunks[chunk][6]
        final = (sums1, sums2)[chunk].at[core]
        wait_total(result.at[pl.ds(0, len(planes[chunk][1]) * pers[chunk])], sem(chunk, 3)[1])
        copy = remote(result, final, *sem(chunk, 4), to_sib)
        copy.start()
        keep = pltpu.make_async_copy(result, final, local_sem.at[12 + chunk])
        keep.start()
        return copy, keep

    def vec_line_start():
        at, peers = lines[1]
        mine = pl.multiple_of(core * 8, 8)
        vec_z[at] = high_low(vector_s[pl.ds(mine, 8), :] + joined(core_recv2[TILES]))
        slot = vec_z.at[at]
        for _, where in peers:
            remote(slot, slot, ar_send.at[10], ar_recv.at[10], where).start()

    def vec_plane_start():
        at, peers = planes[1]
        count = len(lines[1][1])
        wait_total(vec_z.at[pl.ds(0, count)], ar_recv.at[10])
        total = joined(vec_z[0])
        for i in range(1, count + 1):
            total = total + joined(vec_z[i])
        vec_m[at] = high_low(total)
        slot = vec_m.at[at]
        for _, where in peers:
            remote(slot, slot, ar_send.at[11], ar_recv.at[11], where).start()

    def vec_back():
        wait_total(vec_m.at[pl.ds(0, len(planes[1][1]))], ar_recv.at[11])
        total = jnp.sum(vec_m[...].astype(F32), axis=0)
        own_sum2[TILES] = high_low(total[:8] + total[8:])

    def finish(chunk, copies):
        send1, _, recv2, result = chunks[chunk][3:7]
        count = len(planes[chunk][1])
        wait_total(send1.at[pl.ds(0, count)], sem(chunk, 1)[0])
        wait_total(recv2.at[pl.ds(0, len(lines[chunk][1]))], sem(chunk, 2)[0])
        wait_total(result.at[pl.ds(0, count * pers[chunk])], sem(chunk, 3)[0])
        for copy in copies:
            copy.wait()

    project(0)
    first_pass(0)
    block_output(0)
    project_cotangent(0)
    heard_rings()
    second_pass(0, 0)
    second_pass(0, 1)
    forward_terms(0)
    backward_terms(0)
    norm_backward(0)
    project(1)
    first_pass(1)
    block_output(1)
    project_cotangent(1)
    second_pass(1, 0)
    second_pass(1, 1)
    forward_terms(1)
    core_copy1 = core_start(0)
    backward_terms(1)
    core_copy2 = core_start(1)
    heard(len(steps) - 1, steps[-1])
    norm_backward(1)

    def to_z_order(pair, win, stage, result, at):
        for copy in pair:
            copy.wait_recv()
        for p in range(2):
            row = to_s[:, p * PATCH : (p + 1) * PATCH] - offset
            hot = one_hot(row, p * HALF, HALF + LEN)
            at_p = pl.ds(p * PATCH, PATCH)
            stage[at_p, :] = nn(hot, win[pl.ds(p * HALF, HALF + LEN), :]).astype(BF16)
        store = pltpu.make_async_copy(stage, result, local_sem.at[at])
        store.start()
        return store

    m_start(0, core_copy1)
    m_start(1, core_copy2)
    vec_line_start()
    ex_out[1] = to_side(1, out_win, HALF, out_win, 4)
    ex_grad[1] = to_side(1, grad_win, HALF, grad_win, 6)
    z_start(0)
    z_start(1)
    vec_plane_start()
    m_back(0)
    m_back(1)
    store_out = to_z_order(ex_out, out_win, out_stage, output, 10)
    store_grad = to_z_order(ex_grad, grad_win, grad_stage, grad_points, 11)
    vec_back()
    last1 = core_back(0)
    last2 = core_back(1)
    finish(0, last1)
    wait_total(vec_z.at[pl.ds(0, len(lines[1][1]))], ar_send.at[10])
    wait_total(vec_m.at[pl.ds(0, len(planes[1][1]))], ar_send.at[11])
    for pair in (ex_p, ex_c, ex_out, ex_grad):
        for copy in pair:
            copy.wait_send()
    store_out.wait()
    store_grad.wait()
    finish(1, last2)


def results_kernel(
    factor,
    output_in,
    grad_in,
    sums1_in,
    sums2_in,
    output,
    grad_points,
    grad_w_qkv,
    grad_b_qkv,
    grad_w_out,
    grad_b_out,
    grad_gain,
    grad_bias,
    output_s,
    grad_s,
    sums1,
    sums2,
    w_qkv_s,
    w_out_s,
    vec_s,
    in_sems,
    out_sems,
):
    loads = [(sums1_in, sums1), (sums2_in, sums2), (output_in, output_s), (grad_in, grad_s)]
    loads = [pltpu.make_async_copy(a, b, in_sems.at[i]) for i, (a, b) in enumerate(loads)]
    for load in loads:
        load.start()
    stores = []

    def store(a, b):
        stores.append(pltpu.make_async_copy(a, b, out_sems.at[len(stores)]))
        stores[-1].start()

    def block(sums, c, half):
        return sums[c, pl.ds(half * 16, 16)].reshape(256, 128).astype(F32) * factor

    def weight(sums, c, stage, first, result):
        for half in range(2):
            stage[:, pl.ds(first + half * 128, 128)] = block(sums, c, half)
        columns = pl.ds(first, D)
        store(stage.at[:, columns], result.at[:, columns])

    loads[0].wait()
    weight(sums1, 0, w_qkv_s, 512, grad_w_qkv)
    weight(sums1, 1, w_out_s, 0, grad_w_out)
    loads[1].wait()
    weight(sums2, 0, w_qkv_s, 0, grad_w_qkv)
    weight(sums2, 1, w_qkv_s, 256, grad_w_qkv)
    vectors = []
    for c in range(2):
        tile = sums2[c, TILES].astype(F32)
        vectors.append((tile[:8] + tile[8:]) * factor)
    for part in range(6):
        vec_s[0:1, part * 128 : part * 128 + 128] = vectors[0][part : part + 1]
        row = 1 + part // 2
        vec_s[row : row + 1, (part % 2) * 128 : (part % 2) * 128 + 128] = vectors[1][part : part + 1]
    store(vec_s.at[0], grad_b_qkv)
    store(vec_s.at[1, pl.ds(0, D)], grad_b_out)
    store(vec_s.at[2, pl.ds(0, D)], grad_gain)
    store(vec_s.at[3, pl.ds(0, D)], grad_bias)
    loads[2].wait()
    store(output_s, output)
    loads[3].wait()
    store(grad_s, grad_points)
    for copy in stores:
        copy.wait()


def on_device(n_pt, n_case, n_x, n_y, points, cotangent, to_hilbert, from_hilbert, *params):
    plane1, plane2 = n_x * n_y, n_x * n_case
    per1, per2 = TILES // plane1, TILES // plane2
    hbm = pl.BlockSpec(memory_space=pl.ANY)
    shape = jax.ShapeDtypeStruct
    rows = shape((LEN, D), BF16)

    def tiles(*lead):
        return pltpu.VMEM((*lead, 16, 128), BF16)

    output, grad_points, sums1, sums2 = pl.pallas_call(
        functools.partial(kernel, n_pt, n_case, n_x, n_y),
        out_shape=(
            rows,
            rows,
            shape((2, TILES, 16, 128), BF16),
            shape((2, TILES + 1, 16, 128), BF16),
        ),
        in_specs=[hbm] * 10,
        out_specs=(hbm,) * 4,
        scratch_shapes=[
            pltpu.VMEM((1, LEN), jnp.int32),
            pltpu.VMEM((1, LEN), jnp.int32),
            pltpu.VMEM((1, D), F32),
            pltpu.VMEM((1, D), F32),
            pltpu.VMEM((1, 3 * D), F32),
            pltpu.VMEM((1, D), F32),
            pltpu.VMEM((D, 3 * D), BF16),
            pltpu.VMEM((D, D), BF16),
            pltpu.VMEM((WIN, D), BF16),
            pltpu.VMEM((WIN, D), BF16),
            pltpu.VMEM((WIN, D), BF16),
            pltpu.VMEM((WIN, D), BF16),
            pltpu.VMEM((2, PATCH, D), F32),
            pltpu.VMEM((2, PATCH, D), F32),
            pltpu.VMEM((2, PATCH, D), F32),
            pltpu.VMEM((2, PATCH, 128), F32),
            pltpu.VMEM((2, D, PATCH), BF16),
            pltpu.VMEM((2, PATCH, 3 * D), BF16),
            pltpu.VMEM((2, PATCH, D), BF16),
            pltpu.VMEM((8, PATCH, PATCH), F32),
            pltpu.VMEM((2, D, PATCH), BF16),
            pltpu.VMEM((2, PATCH, 3 * D), BF16),
            pltpu.VMEM((PATCH, D), F32),
            pltpu.VMEM((16, 128), F32),
            pltpu.VMEM((2, TILES, 16, 128), F32),
            pltpu.VMEM((2, TILES, 16, 128), F32),
            tiles(TILES),
            tiles(TILES + 1),
            tiles(TILES),
            tiles(TILES + 1),
            tiles(plane1, per1),
            tiles(plane2, per2),
            tiles(plane1, per1),
            tiles(plane2, per2),
            tiles(n_case, per1),
            tiles(n_y, per2),
            tiles(n_y),
            tiles(plane2),
            tiles(TILES),
            tiles(TILES + 1),
            pltpu.VMEM((LEN, D), BF16),
            pltpu.VMEM((LEN, D), BF16),
            pltpu.SemaphoreType.DMA((14,)),
            pltpu.SemaphoreType.DMA((8,)),
            pltpu.SemaphoreType.DMA((8,)),
            pltpu.SemaphoreType.DMA((14,)),
            pltpu.SemaphoreType.DMA((14,)),
            pltpu.SemaphoreType.REGULAR((3,)),
        ],
        compiler_params=pltpu.CompilerParams(
            collective_id=0, has_side_effects=True, vmem_limit_bytes=VMEM_LIMIT
        ),
    )(points[0], cotangent[0], to_hilbert, from_hilbert, *params)
    factor = 1.0 / math.sqrt(n_pt * n_case * LEN)
    result = pl.pallas_call(
        functools.partial(results_kernel, factor),
        out_shape=(
            rows,
            rows,
            shape((D, 3 * D), F32),
            shape((3 * D,), F32),
            shape((D, D), F32),
            shape((D,), F32),
            shape((D,), F32),
            shape((D,), F32),
        ),
        in_specs=[hbm] * 4,
        out_specs=(hbm,) * 8,
        scratch_shapes=[
            pltpu.VMEM((LEN, D), BF16),
            pltpu.VMEM((LEN, D), BF16),
            tiles(2, TILES),
            tiles(2, TILES + 1),
            pltpu.VMEM((D, 3 * D), F32),
            pltpu.VMEM((D, D), F32),
            pltpu.VMEM((4, 3 * D), F32),
            pltpu.SemaphoreType.DMA((4,)),
            pltpu.SemaphoreType.DMA((10,)),
        ],
        compiler_params=pltpu.CompilerParams(vmem_limit_bytes=VMEM_LIMIT),
    )(output, grad_points, sums1, sums2)
    return (result[0][None], result[1][None], *result[2:])


def solution(mesh):
    n_pt, n_case = mesh.shape["pt"], mesh.shape["case"]
    members = n_pt // 2
    n_y = 8 if members >= 32 else 2
    rows = P("case", "pt", None)
    index = P("case", "pt")
    return jax.shard_map(
        functools.partial(on_device, n_pt, n_case, members // n_y, n_y),
        mesh=mesh,
        in_specs=(rows, rows, index, index) + (P(),) * 6,
        out_specs=(rows, rows) + (P(),) * 6,
        check_vma=False,
    )
```

```python
import functools
import math

import jax
import jax.numpy as jnp
from jax import lax
from jax.experimental import pallas as pl
from jax.experimental.pallas import tpu as pltpu
from jax.sharding import PartitionSpec as P

D = 256
HEADS = 8
HEAD = 32
PATCH = 256
LEN = 512
HALF = 256
WIN = 1024
TILES = 32
epsilon = 1e-05
VMEM_LIMIT = 60 * 1024 * 1024
SCALE = 1.0 / math.sqrt(HEAD)
EXP2_SCALE = SCALE * math.log2(math.e)

MESH = pl.DeviceIdType.MESH
F32 = jnp.float32
BF16 = jnp.bfloat16


def nn(a, b):
    return lax.dot_general(a, b, (((1,), (0,)), ((), ())), preferred_element_type=F32)


def nt(a, b):
    return lax.dot_general(a, b, (((1,), (1,)), ((), ())), preferred_element_type=F32)


def one_hot(index_row, low, width):
    columns = [
        jnp.transpose(jnp.broadcast_to(index_row[:, a : a + 128], (128, 128))) for a in (0, 128)
    ]
    column = jnp.concatenate(columns, axis=0) - low
    lane = lax.broadcasted_iota(jnp.int32, (256, 128), 1)
    return jnp.concatenate(
        [jnp.where(column == lane + b, 1.0, 0.0).astype(BF16) for b in range(0, width, 128)],
        axis=1,
    )


def ring_order(n_x, n_y):
    places = [(x, y) for x in range(n_x) for y in range(n_y) if x or y]
    return sorted(places, key=lambda p: -(min(p[0], n_x - p[0]) + min(p[1], n_y - p[1])))


def to_tiles(block):
    return jnp.concatenate([block[:, a : a + 128].reshape(16, 16, 128) for a in (0, 128)], axis=0)


def kernel(
    n_pt,
    n_case,
    n_x,
    n_y,
    points,
    cotangent,
    to_hilbert,
    from_hilbert,
    ln_gain,
    ln_bias,
    w_qkv_in,
    b_qkv,
    w_out_in,
    b_out,
    output,
    grad_points,
    sums1,
    sums2,
    to_s,
    from_s,
    gain_s,
    bias_s,
    b_qkv_s,
    b_out_s,
    w_qkv,
    w_out,
    point_win,
    cot_win,
    out_win,
    grad_win,
    hilbert_p,
    hilbert_c,
    standard_s,
    inverse_s,
    normed_t_s,
    proj_s,
    d_att_s,
    prob_s,
    attended_t_s,
    d_proj_s,
    d_normed_s,
    vector_s,
    acc1,
    acc2,
    core_send1,
    core_send2,
    core_recv1,
    core_recv2,
    m_send1,
    m_send2,
    m_recv1,
    m_recv2,
    z_recv1,
    z_recv2,
    vec_z,
    vec_m,
    own_sum1,
    own_sum2,
    out_stage,
    grad_stage,
    local_sem,
    ex_send,
    ex_recv,
    ar_send,
    ar_recv,
    in_sem,
):
    pt = lax.axis_index("pt")
    case = lax.axis_index("case")
    core = lax.rem(pt, 2)
    member = lax.div(pt, 2)
    sibling = pt + 1 - 2 * core
    outer = lax.rem(pt + n_pt - 1 + 2 * core, n_pt)

    x_at = lax.div(member, n_y)
    y_at = lax.rem(member, n_y)

    def m_peer(place):
        to = lax.rem(x_at + place[0], n_x) * n_y + lax.rem(y_at + place[1], n_y)
        return to, {"pt": to * 2 + core, "case": case}

    def z_peer(r):
        to = lax.rem(case + r, n_case)
        return to, {"pt": pt, "case": to}

    def xz_peer(place):
        x_to = lax.rem(x_at + place[0], n_x)
        z_to = lax.rem(case + place[1], n_case)
        return x_to * n_case + z_to, {"pt": (x_to * n_y + y_at) * 2 + core, "case": z_to}

    def y_peer(r):
        to = lax.rem(y_at + r, n_y)
        return to, {"pt": (x_at * n_y + to) * 2 + core, "case": case}

    xy_peers = [m_peer(place) for place in ring_order(n_x, n_y)]
    z_peers = [z_peer(r) for _, r in ring_order(1, n_case)]
    xz_peers = [xz_peer(place) for place in ring_order(n_x, n_case)]
    y_peers = [y_peer(r) for _, r in ring_order(1, n_y)]
    planes = ((member, xy_peers), (x_at * n_case + case, xz_peers))
    lines = ((case, z_peers), (y_at, y_peers))

    def for_peers(peers, body):
        for peer in peers:
            body(*peer)

    barrier = pltpu.get_barrier_semaphore()

    def signal(_, where):
        pl.semaphore_signal(barrier, inc=1, device_id=where, device_id_type=MESH)

    to_sib = {"pt": sibling, "case": case}
    signal(None, {"pt": outer, "case": case})
    signal(None, to_sib)
    near = [m_peer((0, 1)), m_peer((0, n_y - 1)), m_peer((1, 0)), m_peer((n_x - 1, 0))]
    near += [z_peer(1), z_peer(n_case - 1)]
    for_peers(near, signal)
    loads = [
        (points, point_win.at[pl.ds(HALF, LEN)]),
        (cotangent, cot_win.at[pl.ds(HALF, LEN)]),
        (from_hilbert, from_s),
        (ln_gain, gain_s.at[0]),
        (ln_bias, bias_s.at[0]),
        (w_qkv_in, w_qkv),
        (b_qkv, b_qkv_s.at[0]),
        (w_out_in, w_out),
        (b_out, b_out_s.at[0]),
        (to_hilbert, to_s),
    ]
    loads = [pltpu.make_async_copy(a, b, local_sem.at[i]) for i, (a, b) in enumerate(loads)]
    for load in loads:
        load.start()
    pl.semaphore_wait(barrier, 2 + len(near))

    def tell(step, peers):
        for _, where in peers:
            pl.semaphore_signal(in_sem.at[step], inc=1, device_id=where, device_id_type=MESH)

    def heard(step, peers):
        pl.semaphore_wait(in_sem.at[step], len(peers))

    steps = [near]
    if n_y > 4 or n_case > 4:
        steps.append([m_peer((0, 2)), m_peer((0, n_y - 2)), z_peer(2), z_peer(n_case - 2)])
    steps.append([m_peer((dx, 0)) for dx in range(1, n_x)])
    tell(0, steps[0])

    def remote(src, dst, send_sem, recv_sem, where):
        return pltpu.make_async_remote_copy(
            src_ref=src,
            dst_ref=dst,
            send_sem=send_sem,
            recv_sem=recv_sem,
            device_id=where,
            device_id_type=MESH,
        )

    halves = (1 - core, core)

    def rows_of(p, first=0):
        return pl.ds(pl.multiple_of(first + p * PATCH, PATCH), PATCH)

    def side_rows(p):
        return pl.ds(pl.multiple_of(p * (HALF + LEN), HALF), HALF)

    def to_side(i, src, first_row, win, at):
        where = to_sib if i == 0 else {"pt": outer, "case": case}
        p = halves[i]
        copy = remote(
            src.at[rows_of(p, first_row)],
            win.at[side_rows(1 - p)],
            ex_send.at[at + i],
            ex_recv.at[at + i],
            where,
        )
        copy.start()
        return copy

    ex_p = [to_side(i, points, 0, point_win, 0) for i in (1, 0)][::-1]
    ex_c = [to_side(i, cotangent, 0, cot_win, 2) for i in (1, 0)][::-1]
    ex_out = [None, None]
    ex_grad = [None, None]

    own = pl.ds(HALF, LEN)
    offset = pt * LEN - HALF

    for load in loads[:3]:
        load.wait()
    hots = []
    for i, p in enumerate(halves):
        row = from_s[:, rows_of(p)] - offset
        hot = one_hot(row, HALF, LEN)
        hilbert_p[i] = nn(hot, point_win[own, :])
        hilbert_c[i] = nn(hot, cot_win[own, :])
        hots.append(one_hot(row, p * (HALF + LEN), HALF))
    for load in loads[3:]:
        load.wait()
    heard(0, steps[0])
    tell(1, steps[1])

    def heard_rings():
        if len(steps) == 3:
            heard(1, steps[1])
            tell(2, steps[2])

    gain = gain_s[...]
    lane_head = lax.broadcasted_iota(jnp.int32, (1, 128), 1) // HEAD
    masks = [jnp.where(lane_head == h, 1.0, 0.0).astype(BF16) for h in range(4)]

    def project(i):
        p = halves[i]
        ex_p[i].wait_recv()
        features = hilbert_p[i] + nn(hots[i], point_win[side_rows(p), :])
        hilbert_p[i] = features
        centered = features - jnp.mean(features, axis=-1, keepdims=True)
        inverse = lax.rsqrt(jnp.mean(centered * centered, axis=-1, keepdims=True) + epsilon)
        standard = centered * inverse
        standard_s[i] = standard
        inverse_s[i] = jnp.broadcast_to(inverse, (PATCH, 128))
        normed = (standard * gain + bias_s[...]).astype(BF16)
        normed_t_s[i] = jnp.transpose(normed)
        proj_s[i] = (nn(normed, w_qkv[...]) + b_qkv_s[...]).astype(BF16)

    def project_cotangent(i):
        p = halves[i]
        ex_c[i].wait_recv()
        cot = hilbert_c[i] + nn(hots[i], cot_win[side_rows(p), :])
        hilbert_c[i] = cot
        d_att_s[i] = nt(cot.astype(BF16), w_out[...]).astype(BF16)

    def first_pass(i):
        def scores(unit):
            b0 = unit // 4 * 128
            k = proj_s[i, :, pl.ds(256 + b0, 128)]
            return nt(k * masks[unit % 4], proj_s[i, :, pl.ds(b0, 128)])

        ahead = [scores(unit) for unit in range(4)]
        for unit in range(HEADS):
            if unit + 4 < HEADS:
                ahead.append(scores(unit + 4))
            if unit % 4 == 0:
                v_t = jnp.transpose(proj_s[i, :, pl.ds(512 + unit // 4 * 128, 128)])
            h = unit % 4
            exponent = jnp.exp2(ahead[unit] * EXP2_SCALE)
            total = jnp.sum(exponent, axis=0, keepdims=True)
            prob = exponent * (1.0 / total)
            prob_s[unit] = prob
            att_t = nn(v_t[h * HEAD : (h + 1) * HEAD], prob.astype(BF16))
            attended_t_s[i, pl.ds(unit * HEAD, HEAD), :] = att_t.astype(BF16)

    def block_output(i):
        attended = jnp.transpose(attended_t_s[i])
        branch = nn(attended, w_out[...]) + b_out_s[...]
        out_win[rows_of(halves[i], HALF), :] = (hilbert_p[i] + branch).astype(BF16)
        if i == 0:
            ex_out[i] = to_side(i, out_win, HALF, out_win, 4)

    def second_pass(i):
        def d_probs(unit):
            b0 = unit // 4 * 128
            v = proj_s[i, :, pl.ds(512 + b0, 128)]
            return nt(v * masks[unit % 4], d_att_s[i, :, pl.ds(b0, 128)])

        def d_scores(unit):
            prob, d_prob = prob_s[unit], ahead[unit]
            row_sum = jnp.sum(prob * d_prob, axis=0, keepdims=True)
            return (prob * (d_prob - row_sum) * SCALE).astype(BF16)

        ahead = [d_probs(unit) for unit in range(4)]
        low = [d_scores(0)]
        for unit in range(HEADS):
            h, b0 = unit % 4, unit // 4 * 128
            if unit + 4 < HEADS:
                ahead.append(d_probs(unit + 4))
            if unit + 1 < HEADS:
                low.append(d_scores(unit + 1))
            if h == 0:
                q = proj_s[i, :, pl.ds(b0, 128)]
                k_t = jnp.transpose(proj_s[i, :, pl.ds(256 + b0, 128)])
                da = d_att_s[i, :, pl.ds(b0, 128)]
                d_q_t = []
            d_v_h = nn(prob_s[unit].astype(BF16), da * masks[h])
            d_k_h = nn(low[unit], q * masks[h])
            d_v = d_v_h if h == 0 else d_v + d_v_h
            d_k = d_k_h if h == 0 else d_k + d_k_h
            d_q_t.append(nn(k_t[h * HEAD : (h + 1) * HEAD], low[unit]))
            if h == 3:
                d_q = jnp.transpose(jnp.concatenate(d_q_t, axis=0))
                d_proj_s[i, :, pl.ds(b0, 128)] = d_q.astype(BF16)
                d_proj_s[i, :, pl.ds(256 + b0, 128)] = d_k.astype(BF16)
                d_proj_s[i, :, pl.ds(512 + b0, 128)] = d_v.astype(BF16)

    def add(ref, index, value, i):
        ref[index] = value if i == 0 else ref[index] + value

    def forward_terms(i):
        d_v = d_proj_s[i, :, pl.ds(512, 256)]
        add(acc1, 0, to_tiles(nn(normed_t_s[i], d_v)), i)
        add(acc1, 1, to_tiles(nn(attended_t_s[i], hilbert_c[i].astype(BF16))), i)

    def backward_terms(i):
        d_proj = d_proj_s[i]
        d_normed = nt(d_proj, w_qkv[...])
        d_normed_s[...] = d_normed
        sums = (
            (0, jnp.sum(d_proj.astype(F32), axis=0, keepdims=True)),
            (8, jnp.sum(hilbert_c[i], axis=0, keepdims=True)),
            (10, jnp.sum(d_normed * standard_s[i], axis=0, keepdims=True)),
            (12, jnp.sum(d_normed, axis=0, keepdims=True)),
        )
        if i == 0:
            vector_s[...] = jnp.zeros((16, 128), F32)
        for row, value in sums:
            for part in range(value.shape[1] // 128):
                add(
                    vector_s,
                    slice(row + part, row + part + 1),
                    value[:, part * 128 : part * 128 + 128],
                    i,
                )
        add(acc2, 0, to_tiles(nn(normed_t_s[i], d_proj[:, :256])), i)
        add(acc2, 1, to_tiles(nn(normed_t_s[i], d_proj[:, 256:512])), i)

    def norm_backward(i):
        d_normed = d_normed_s[...]
        standard = standard_s[i]
        scaled = d_normed * gain
        inverse = inverse_s[i]
        inverse = jnp.concatenate([inverse, inverse], axis=1)
        d_input = inverse * (
            scaled
            - jnp.mean(scaled, axis=-1, keepdims=True)
            - standard * jnp.mean(scaled * standard, axis=-1, keepdims=True)
        )
        grad_win[rows_of(halves[i], HALF), :] = (hilbert_c[i] + d_input).astype(BF16)
        if i == 0:
            ex_grad[i] = to_side(i, grad_win, HALF, grad_win, 6)

    chunks = (
        (acc1, core_send1, core_recv1, m_send1, m_recv1, z_recv1, own_sum1),
        (acc2, core_send2, core_recv2, m_send2, m_recv2, z_recv2, own_sum2),
    )
    pers = (TILES // (n_x * n_y), TILES // (n_x * n_case))

    def sem(chunk, stage):
        return ar_send.at[chunk * 5 + stage], ar_recv.at[chunk * 5 + stage]

    def wait_total(ref, semaphore):
        pltpu.make_async_copy(ref, ref, semaphore).wait()

    def high_low(value):
        high = value.astype(BF16)
        low = (value - high.astype(F32)).astype(BF16)
        return jnp.concatenate([high, low], axis=0)

    def joined(tile):
        tile = tile.astype(F32)
        return tile[:8] + tile[8:]

    def core_start(chunk):
        acc, send, recv = chunks[chunk][:3]
        send[pl.ds(0, TILES)] = acc[1 - core].astype(BF16)
        if chunk:
            theirs = pl.multiple_of((1 - core) * 8, 8)
            send[TILES] = high_low(vector_s[pl.ds(theirs, 8), :])
        copy = remote(send, recv, *sem(chunk, 0), to_sib)
        copy.start()
        return copy

    def m_start(chunk, copy):
        acc, _, recv0, send, recv = chunks[chunk][:5]
        at, peers = planes[chunk]
        copy.wait()
        half = (acc[core] + recv0[pl.ds(0, TILES)].astype(F32)).astype(BF16)
        send[...] = half.reshape(len(peers) + 1, pers[chunk], 16, 128)
        recv[pl.ds(at, 1)] = send[pl.ds(at, 1)]
        s, r = sem(chunk, 1)
        for to, where in peers:
            remote(send.at[to], recv.at[at], s, r, where).start()

    def z_start(chunk):
        recv0, recv = chunks[chunk][4:6]
        at, peers = lines[chunk]
        wait_total(recv0.at[pl.ds(0, len(planes[chunk][1]))], sem(chunk, 1)[1])
        recv[at] = jnp.sum(recv0[...].astype(F32), axis=0).astype(BF16)
        s, r = sem(chunk, 2)
        slot = recv.at[at]
        for _, where in peers:
            remote(slot, slot, s, r, where).start()

    def m_back(chunk):
        recv0, result = chunks[chunk][5:7]
        at, peers = planes[chunk]
        wait_total(recv0.at[pl.ds(0, len(lines[chunk][1]))], sem(chunk, 2)[1])
        rows = pl.ds(at * pers[chunk], pers[chunk])
        result[rows] = jnp.sum(recv0[...].astype(F32), axis=0).astype(BF16)
        s, r = sem(chunk, 3)
        slot = result.at[rows]
        for _, where in peers:
            remote(slot, slot, s, r, where).start()

    def core_back(chunk):
        result = chunks[chunk][6]
        final = (sums1, sums2)[chunk].at[core]
        wait_total(result.at[pl.ds(0, len(planes[chunk][1]) * pers[chunk])], sem(chunk, 3)[1])
        copy = remote(result, final, *sem(chunk, 4), to_sib)
        copy.start()
        keep = pltpu.make_async_copy(result, final, local_sem.at[12 + chunk])
        keep.start()
        return copy, keep

    def vec_line_start():
        at, peers = lines[1]
        mine = pl.multiple_of(core * 8, 8)
        vec_z[at] = high_low(vector_s[pl.ds(mine, 8), :] + joined(core_recv2[TILES]))
        slot = vec_z.at[at]
        for _, where in peers:
            remote(slot, slot, ar_send.at[10], ar_recv.at[10], where).start()

    def vec_plane_start():
        at, peers = planes[1]
        count = len(lines[1][1])
        wait_total(vec_z.at[pl.ds(0, count)], ar_recv.at[10])
        total = joined(vec_z[0])
        for i in range(1, count + 1):
            total = total + joined(vec_z[i])
        vec_m[at] = high_low(total)
        slot = vec_m.at[at]
        for _, where in peers:
            remote(slot, slot, ar_send.at[11], ar_recv.at[11], where).start()

    def vec_back():
        wait_total(vec_m.at[pl.ds(0, len(planes[1][1]))], ar_recv.at[11])
        total = jnp.sum(vec_m[...].astype(F32), axis=0)
        own_sum2[TILES] = high_low(total[:8] + total[8:])

    def finish(chunk, copies):
        send1, _, recv2, result = chunks[chunk][3:7]
        count = len(planes[chunk][1])
        wait_total(send1.at[pl.ds(0, count)], sem(chunk, 1)[0])
        wait_total(recv2.at[pl.ds(0, len(lines[chunk][1]))], sem(chunk, 2)[0])
        wait_total(result.at[pl.ds(0, count * pers[chunk])], sem(chunk, 3)[0])
        for copy in copies:
            copy.wait()

    project(0)
    first_pass(0)
    block_output(0)
    project_cotangent(0)
    heard_rings()
    second_pass(0)
    forward_terms(0)
    backward_terms(0)
    norm_backward(0)
    project(1)
    first_pass(1)
    block_output(1)
    project_cotangent(1)
    second_pass(1)
    forward_terms(1)
    core_copy1 = core_start(0)
    backward_terms(1)
    core_copy2 = core_start(1)
    heard(len(steps) - 1, steps[-1])
    norm_backward(1)

    def to_z_order(pair, win, stage, result, at):
        for copy in pair:
            copy.wait_recv()
        for p in range(2):
            row = to_s[:, p * PATCH : (p + 1) * PATCH] - offset
            hot = one_hot(row, p * HALF, HALF + LEN)
            at_p = pl.ds(p * PATCH, PATCH)
            stage[at_p, :] = nn(hot, win[pl.ds(p * HALF, HALF + LEN), :]).astype(BF16)
        store = pltpu.make_async_copy(stage, result, local_sem.at[at])
        store.start()
        return store

    m_start(0, core_copy1)
    m_start(1, core_copy2)
    vec_line_start()
    ex_out[1] = to_side(1, out_win, HALF, out_win, 4)
    ex_grad[1] = to_side(1, grad_win, HALF, grad_win, 6)
    z_start(0)
    z_start(1)
    vec_plane_start()
    m_back(0)
    m_back(1)
    store_out = to_z_order(ex_out, out_win, out_stage, output, 10)
    store_grad = to_z_order(ex_grad, grad_win, grad_stage, grad_points, 11)
    vec_back()
    last1 = core_back(0)
    last2 = core_back(1)
    finish(0, last1)
    wait_total(vec_z.at[pl.ds(0, len(lines[1][1]))], ar_send.at[10])
    wait_total(vec_m.at[pl.ds(0, len(planes[1][1]))], ar_send.at[11])
    for pair in (ex_p, ex_c, ex_out, ex_grad):
        for copy in pair:
            copy.wait_send()
    store_out.wait()
    store_grad.wait()
    finish(1, last2)


def results_kernel(
    factor,
    output_in,
    grad_in,
    sums1_in,
    sums2_in,
    output,
    grad_points,
    grad_w_qkv,
    grad_b_qkv,
    grad_w_out,
    grad_b_out,
    grad_gain,
    grad_bias,
    output_s,
    grad_s,
    sums1,
    sums2,
    w_qkv_s,
    w_out_s,
    vec_s,
    in_sems,
    out_sems,
):
    loads = [(sums1_in, sums1), (sums2_in, sums2), (output_in, output_s), (grad_in, grad_s)]
    loads = [pltpu.make_async_copy(a, b, in_sems.at[i]) for i, (a, b) in enumerate(loads)]
    for load in loads:
        load.start()
    stores = []

    def store(a, b):
        stores.append(pltpu.make_async_copy(a, b, out_sems.at[len(stores)]))
        stores[-1].start()

    def block(sums, c, half):
        return sums[c, pl.ds(half * 16, 16)].reshape(256, 128).astype(F32) * factor

    def weight(sums, c, stage, first, result):
        for half in range(2):
            stage[:, pl.ds(first + half * 128, 128)] = block(sums, c, half)
        columns = pl.ds(first, D)
        store(stage.at[:, columns], result.at[:, columns])

    loads[0].wait()
    weight(sums1, 0, w_qkv_s, 512, grad_w_qkv)
    weight(sums1, 1, w_out_s, 0, grad_w_out)
    loads[1].wait()
    weight(sums2, 0, w_qkv_s, 0, grad_w_qkv)
    weight(sums2, 1, w_qkv_s, 256, grad_w_qkv)
    vectors = []
    for c in range(2):
        tile = sums2[c, TILES].astype(F32)
        vectors.append((tile[:8] + tile[8:]) * factor)
    for part in range(6):
        vec_s[0:1, part * 128 : part * 128 + 128] = vectors[0][part : part + 1]
        row = 1 + part // 2
        vec_s[row : row + 1, (part % 2) * 128 : (part % 2) * 128 + 128] = vectors[1][part : part + 1]
    store(vec_s.at[0], grad_b_qkv)
    store(vec_s.at[1, pl.ds(0, D)], grad_b_out)
    store(vec_s.at[2, pl.ds(0, D)], grad_gain)
    store(vec_s.at[3, pl.ds(0, D)], grad_bias)
    loads[2].wait()
    store(output_s, output)
    loads[3].wait()
    store(grad_s, grad_points)
    for copy in stores:
        copy.wait()


def on_device(n_pt, n_case, n_x, n_y, points, cotangent, to_hilbert, from_hilbert, *params):
    plane1, plane2 = n_x * n_y, n_x * n_case
    per1, per2 = TILES // plane1, TILES // plane2
    hbm = pl.BlockSpec(memory_space=pl.ANY)
    shape = jax.ShapeDtypeStruct
    rows = shape((LEN, D), BF16)

    def tiles(*lead):
        return pltpu.VMEM((*lead, 16, 128), BF16)

    output, grad_points, sums1, sums2 = pl.pallas_call(
        functools.partial(kernel, n_pt, n_case, n_x, n_y),
        out_shape=(
            rows,
            rows,
            shape((2, TILES, 16, 128), BF16),
            shape((2, TILES + 1, 16, 128), BF16),
        ),
        in_specs=[hbm] * 10,
        out_specs=(hbm,) * 4,
        scratch_shapes=[
            pltpu.VMEM((1, LEN), jnp.int32),
            pltpu.VMEM((1, LEN), jnp.int32),
            pltpu.VMEM((1, D), F32),
            pltpu.VMEM((1, D), F32),
            pltpu.VMEM((1, 3 * D), F32),
            pltpu.VMEM((1, D), F32),
            pltpu.VMEM((D, 3 * D), BF16),
            pltpu.VMEM((D, D), BF16),
            pltpu.VMEM((WIN, D), BF16),
            pltpu.VMEM((WIN, D), BF16),
            pltpu.VMEM((WIN, D), BF16),
            pltpu.VMEM((WIN, D), BF16),
            pltpu.VMEM((2, PATCH, D), F32),
            pltpu.VMEM((2, PATCH, D), F32),
            pltpu.VMEM((2, PATCH, D), F32),
            pltpu.VMEM((2, PATCH, 128), F32),
            pltpu.VMEM((2, D, PATCH), BF16),
            pltpu.VMEM((2, PATCH, 3 * D), BF16),
            pltpu.VMEM((2, PATCH, D), BF16),
            pltpu.VMEM((8, PATCH, PATCH), F32),
            pltpu.VMEM((2, D, PATCH), BF16),
            pltpu.VMEM((2, PATCH, 3 * D), BF16),
            pltpu.VMEM((PATCH, D), F32),
            pltpu.VMEM((16, 128), F32),
            pltpu.VMEM((2, TILES, 16, 128), F32),
            pltpu.VMEM((2, TILES, 16, 128), F32),
            tiles(TILES),
            tiles(TILES + 1),
            tiles(TILES),
            tiles(TILES + 1),
            tiles(plane1, per1),
            tiles(plane2, per2),
            tiles(plane1, per1),
            tiles(plane2, per2),
            tiles(n_case, per1),
            tiles(n_y, per2),
            tiles(n_y),
            tiles(plane2),
            tiles(TILES),
            tiles(TILES + 1),
            pltpu.VMEM((LEN, D), BF16),
            pltpu.VMEM((LEN, D), BF16),
            pltpu.SemaphoreType.DMA((14,)),
            pltpu.SemaphoreType.DMA((8,)),
            pltpu.SemaphoreType.DMA((8,)),
            pltpu.SemaphoreType.DMA((14,)),
            pltpu.SemaphoreType.DMA((14,)),
            pltpu.SemaphoreType.REGULAR((3,)),
        ],
        compiler_params=pltpu.CompilerParams(
            collective_id=0, has_side_effects=True, vmem_limit_bytes=VMEM_LIMIT
        ),
    )(points[0], cotangent[0], to_hilbert, from_hilbert, *params)
    factor = 1.0 / math.sqrt(n_pt * n_case * LEN)
    result = pl.pallas_call(
        functools.partial(results_kernel, factor),
        out_shape=(
            rows,
            rows,
            shape((D, 3 * D), F32),
            shape((3 * D,), F32),
            shape((D, D), F32),
            shape((D,), F32),
            shape((D,), F32),
            shape((D,), F32),
        ),
        in_specs=[hbm] * 4,
        out_specs=(hbm,) * 8,
        scratch_shapes=[
            pltpu.VMEM((LEN, D), BF16),
            pltpu.VMEM((LEN, D), BF16),
            tiles(2, TILES),
            tiles(2, TILES + 1),
            pltpu.VMEM((D, 3 * D), F32),
            pltpu.VMEM((D, D), F32),
            pltpu.VMEM((4, 3 * D), F32),
            pltpu.SemaphoreType.DMA((4,)),
            pltpu.SemaphoreType.DMA((10,)),
        ],
        compiler_params=pltpu.CompilerParams(vmem_limit_bytes=VMEM_LIMIT),
    )(output, grad_points, sums1, sums2)
    return (result[0][None], result[1][None], *result[2:])


def solution(mesh):
    n_pt, n_case = mesh.shape["pt"], mesh.shape["case"]
    members = n_pt // 2
    n_y = 8 if members >= 32 else 2
    rows = P("case", "pt", None)
    index = P("case", "pt")
    return jax.shard_map(
        functools.partial(on_device, n_pt, n_case, members // n_y, n_y),
        mesh=mesh,
        in_specs=(rows, rows, index, index) + (P(),) * 6,
        out_specs=(rows, rows) + (P(),) * 6,
        check_vma=False,
    )
```

```python
import functools
import math

import jax
import jax.numpy as jnp
from jax import lax
from jax.experimental import pallas as pl
from jax.experimental.pallas import tpu as pltpu
from jax.sharding import PartitionSpec as P

D = 256
HEADS = 8
HEAD = 32
PATCH = 256
LEN = 512
HALF = 256
WIN = 1024
TILES = 32
epsilon = 1e-05
VMEM_LIMIT = 60 * 1024 * 1024
SCALE = 1.0 / math.sqrt(HEAD)
EXP2_SCALE = SCALE * math.log2(math.e)

MESH = pl.DeviceIdType.MESH
F32 = jnp.float32
BF16 = jnp.bfloat16


def nn(a, b):
    return lax.dot_general(a, b, (((1,), (0,)), ((), ())), preferred_element_type=F32)


def nt(a, b):
    return lax.dot_general(a, b, (((1,), (1,)), ((), ())), preferred_element_type=F32)


def one_hot(index_row, low, width):
    columns = [
        jnp.transpose(jnp.broadcast_to(index_row[:, a : a + 128], (128, 128))) for a in (0, 128)
    ]
    column = jnp.concatenate(columns, axis=0) - low
    lane = lax.broadcasted_iota(jnp.int32, (256, 128), 1)
    return jnp.concatenate(
        [jnp.where(column == lane + b, 1.0, 0.0).astype(BF16) for b in range(0, width, 128)],
        axis=1,
    )


def ring_order(n_x, n_y):
    places = [(x, y) for x in range(n_x) for y in range(n_y) if x or y]
    return sorted(places, key=lambda p: -(min(p[0], n_x - p[0]) + min(p[1], n_y - p[1])))


def to_tiles(block):
    return jnp.concatenate([block[:, a : a + 128].reshape(16, 16, 128) for a in (0, 128)], axis=0)


def kernel(
    n_pt,
    n_case,
    n_x,
    n_y,
    points,
    cotangent,
    to_hilbert,
    from_hilbert,
    ln_gain,
    ln_bias,
    w_qkv_in,
    b_qkv,
    w_out_in,
    b_out,
    output,
    grad_points,
    sums1,
    sums2,
    to_s,
    from_s,
    gain_s,
    bias_s,
    b_qkv_s,
    b_out_s,
    w_qkv,
    w_out,
    point_win,
    cot_win,
    out_win,
    grad_win,
    hilbert_p,
    hilbert_c,
    standard_s,
    inverse_s,
    normed_t_s,
    proj_s,
    d_att_s,
    prob_s,
    attended_t_s,
    d_proj_s,
    d_normed_s,
    vector_s,
    acc1,
    acc2,
    core_send1,
    core_send2,
    core_recv1,
    core_recv2,
    m_send1,
    m_send2,
    m_recv1,
    m_recv2,
    z_recv1,
    z_recv2,
    vec_z,
    vec_m,
    own_sum1,
    own_sum2,
    out_stage,
    grad_stage,
    local_sem,
    ex_send,
    ex_recv,
    ar_send,
    ar_recv,
    in_sem,
):
    pt = lax.axis_index("pt")
    case = lax.axis_index("case")
    core = lax.rem(pt, 2)
    member = lax.div(pt, 2)
    sibling = pt + 1 - 2 * core
    outer = lax.rem(pt + n_pt - 1 + 2 * core, n_pt)

    x_at = lax.div(member, n_y)
    y_at = lax.rem(member, n_y)

    def m_peer(place):
        to = lax.rem(x_at + place[0], n_x) * n_y + lax.rem(y_at + place[1], n_y)
        return to, {"pt": to * 2 + core, "case": case}

    def z_peer(r):
        to = lax.rem(case + r, n_case)
        return to, {"pt": pt, "case": to}

    def xz_peer(place):
        x_to = lax.rem(x_at + place[0], n_x)
        z_to = lax.rem(case + place[1], n_case)
        return x_to * n_case + z_to, {"pt": (x_to * n_y + y_at) * 2 + core, "case": z_to}

    def y_peer(r):
        to = lax.rem(y_at + r, n_y)
        return to, {"pt": (x_at * n_y + to) * 2 + core, "case": case}

    xy_peers = [m_peer(place) for place in ring_order(n_x, n_y)]
    z_peers = [z_peer(r) for _, r in ring_order(1, n_case)]
    xz_peers = [xz_peer(place) for place in ring_order(n_x, n_case)]
    y_peers = [y_peer(r) for _, r in ring_order(1, n_y)]
    planes = ((member, xy_peers), (x_at * n_case + case, xz_peers))
    lines = ((case, z_peers), (y_at, y_peers))

    def for_peers(peers, body):
        for peer in peers:
            body(*peer)

    barrier = pltpu.get_barrier_semaphore()

    def signal(_, where):
        pl.semaphore_signal(barrier, inc=1, device_id=where, device_id_type=MESH)

    to_sib = {"pt": sibling, "case": case}
    signal(None, {"pt": outer, "case": case})
    signal(None, to_sib)
    near = [m_peer((0, 1)), m_peer((0, n_y - 1)), m_peer((1, 0)), m_peer((n_x - 1, 0))]
    near += [z_peer(1), z_peer(n_case - 1)]
    for_peers(near, signal)
    loads = [
        (points, point_win.at[pl.ds(HALF, LEN)]),
        (cotangent, cot_win.at[pl.ds(HALF, LEN)]),
        (from_hilbert, from_s),
        (ln_gain, gain_s.at[0]),
        (ln_bias, bias_s.at[0]),
        (w_qkv_in, w_qkv),
        (b_qkv, b_qkv_s.at[0]),
        (w_out_in, w_out),
        (b_out, b_out_s.at[0]),
        (to_hilbert, to_s),
    ]
    loads = [pltpu.make_async_copy(a, b, local_sem.at[i]) for i, (a, b) in enumerate(loads)]
    for load in loads:
        load.start()
    pl.semaphore_wait(barrier, 2 + len(near))

    def tell(step, peers):
        for _, where in peers:
            pl.semaphore_signal(in_sem.at[step], inc=1, device_id=where, device_id_type=MESH)

    def heard(step, peers):
        pl.semaphore_wait(in_sem.at[step], len(peers))

    steps = [near]
    if n_y > 4 or n_case > 4:
        steps.append([m_peer((0, 2)), m_peer((0, n_y - 2)), z_peer(2), z_peer(n_case - 2)])
    steps.append([m_peer((dx, 0)) for dx in range(1, n_x)])
    tell(0, steps[0])

    def remote(src, dst, send_sem, recv_sem, where):
        return pltpu.make_async_remote_copy(
            src_ref=src,
            dst_ref=dst,
            send_sem=send_sem,
            recv_sem=recv_sem,
            device_id=where,
            device_id_type=MESH,
        )

    halves = (1 - core, core)

    def rows_of(p, first=0):
        return pl.ds(pl.multiple_of(first + p * PATCH, PATCH), PATCH)

    def side_rows(p):
        return pl.ds(pl.multiple_of(p * (HALF + LEN), HALF), HALF)

    def to_side(i, src, first_row, win, at):
        where = to_sib if i == 0 else {"pt": outer, "case": case}
        p = halves[i]
        copy = remote(
            src.at[rows_of(p, first_row)],
            win.at[side_rows(1 - p)],
            ex_send.at[at + i],
            ex_recv.at[at + i],
            where,
        )
        copy.start()
        return copy

    ex_p = [to_side(i, points, 0, point_win, 0) for i in (1, 0)][::-1]
    ex_c = [to_side(i, cotangent, 0, cot_win, 2) for i in (1, 0)][::-1]
    ex_out = [None, None]
    ex_grad = [None, None]

    own = pl.ds(HALF, LEN)
    offset = pt * LEN - HALF

    for load in loads[:3]:
        load.wait()
    hots = []
    for i, p in enumerate(halves):
        row = from_s[:, rows_of(p)] - offset
        hot = one_hot(row, HALF, LEN)
        hilbert_p[i] = nn(hot, point_win[own, :])
        hilbert_c[i] = nn(hot, cot_win[own, :])
        hots.append(one_hot(row, p * (HALF + LEN), HALF))
    for load in loads[3:]:
        load.wait()
    heard(0, steps[0])
    tell(1, steps[1])

    def heard_rings():
        if len(steps) == 3:
            heard(1, steps[1])
            tell(2, steps[2])

    gain = gain_s[...]
    lane_head = lax.broadcasted_iota(jnp.int32, (1, 128), 1) // HEAD
    masks = [jnp.where(lane_head == h, 1.0, 0.0).astype(BF16) for h in range(4)]

    def project(i):
        p = halves[i]
        ex_p[i].wait_recv()
        features = hilbert_p[i] + nn(hots[i], point_win[side_rows(p), :])
        hilbert_p[i] = features
        centered = features - jnp.mean(features, axis=-1, keepdims=True)
        inverse = lax.rsqrt(jnp.mean(centered * centered, axis=-1, keepdims=True) + epsilon)
        standard = centered * inverse
        standard_s[i] = standard
        inverse_s[i] = jnp.broadcast_to(inverse, (PATCH, 128))
        normed = (standard * gain + bias_s[...]).astype(BF16)
        normed_t_s[i] = jnp.transpose(normed)
        proj_s[i] = (nn(normed, w_qkv[...]) + b_qkv_s[...]).astype(BF16)

    def project_cotangent(i):
        p = halves[i]
        ex_c[i].wait_recv()
        cot = hilbert_c[i] + nn(hots[i], cot_win[side_rows(p), :])
        hilbert_c[i] = cot
        d_att_s[i] = nt(cot.astype(BF16), w_out[...]).astype(BF16)

    def first_pass(i):
        def scores(unit):
            b0 = unit // 4 * 128
            k = proj_s[i, :, pl.ds(256 + b0, 128)]
            return nt(k * masks[unit % 4], proj_s[i, :, pl.ds(b0, 128)])

        ahead = [scores(unit) for unit in range(6)]
        for unit in range(HEADS):
            if unit + 6 < HEADS:
                ahead.append(scores(unit + 6))
            if unit % 4 == 0:
                v_t = jnp.transpose(proj_s[i, :, pl.ds(512 + unit // 4 * 128, 128)])
            h = unit % 4
            exponent = jnp.exp2(ahead[unit] * EXP2_SCALE)
            total = jnp.sum(exponent, axis=0, keepdims=True)
            prob = exponent * (1.0 / total)
            prob_s[unit] = prob
            att_t = nn(v_t[h * HEAD : (h + 1) * HEAD], prob.astype(BF16))
            attended_t_s[i, pl.ds(unit * HEAD, HEAD), :] = att_t.astype(BF16)

    def block_output(i):
        attended = jnp.transpose(attended_t_s[i])
        branch = nn(attended, w_out[...]) + b_out_s[...]
        out_win[rows_of(halves[i], HALF), :] = (hilbert_p[i] + branch).astype(BF16)
        if i == 0:
            ex_out[i] = to_side(i, out_win, HALF, out_win, 4)

    def second_pass(i):
        def d_probs(unit):
            b0 = unit // 4 * 128
            v = proj_s[i, :, pl.ds(512 + b0, 128)]
            return nt(v * masks[unit % 4], d_att_s[i, :, pl.ds(b0, 128)])

        def d_scores(unit):
            prob, d_prob = prob_s[unit], ahead[unit]
            row_sum = jnp.sum(prob * d_prob, axis=0, keepdims=True)
            return (prob * (d_prob - row_sum) * SCALE).astype(BF16)

        ahead = [d_probs(unit) for unit in range(6)]
        low = [d_scores(0)]
        for unit in range(HEADS):
            h, b0 = unit % 4, unit // 4 * 128
            if unit + 6 < HEADS:
                ahead.append(d_probs(unit + 6))
            if unit + 1 < HEADS:
                low.append(d_scores(unit + 1))
            if h == 0:
                q = proj_s[i, :, pl.ds(b0, 128)]
                k_t = jnp.transpose(proj_s[i, :, pl.ds(256 + b0, 128)])
                da = d_att_s[i, :, pl.ds(b0, 128)]
                d_q_t = []
            d_v_h = nn(prob_s[unit].astype(BF16), da * masks[h])
            d_k_h = nn(low[unit], q * masks[h])
            d_v = d_v_h if h == 0 else d_v + d_v_h
            d_k = d_k_h if h == 0 else d_k + d_k_h
            d_q_t.append(nn(k_t[h * HEAD : (h + 1) * HEAD], low[unit]))
            if h == 3:
                d_q = jnp.transpose(jnp.concatenate(d_q_t, axis=0))
                d_proj_s[i, :, pl.ds(b0, 128)] = d_q.astype(BF16)
                d_proj_s[i, :, pl.ds(256 + b0, 128)] = d_k.astype(BF16)
                d_proj_s[i, :, pl.ds(512 + b0, 128)] = d_v.astype(BF16)

    def add(ref, index, value, i):
        ref[index] = value if i == 0 else ref[index] + value

    def forward_terms(i):
        d_v = d_proj_s[i, :, pl.ds(512, 256)]
        add(acc1, 0, to_tiles(nn(normed_t_s[i], d_v)), i)
        add(acc1, 1, to_tiles(nn(attended_t_s[i], hilbert_c[i].astype(BF16))), i)

    def backward_terms(i):
        d_proj = d_proj_s[i]
        d_normed = nt(d_proj, w_qkv[...])
        d_normed_s[...] = d_normed
        sums = (
            (0, jnp.sum(d_proj.astype(F32), axis=0, keepdims=True)),
            (8, jnp.sum(hilbert_c[i], axis=0, keepdims=True)),
            (10, jnp.sum(d_normed * standard_s[i], axis=0, keepdims=True)),
            (12, jnp.sum(d_normed, axis=0, keepdims=True)),
        )
        if i == 0:
            vector_s[...] = jnp.zeros((16, 128), F32)
        for row, value in sums:
            for part in range(value.shape[1] // 128):
                add(
                    vector_s,
                    slice(row + part, row + part + 1),
                    value[:, part * 128 : part * 128 + 128],
                    i,
                )
        add(acc2, 0, to_tiles(nn(normed_t_s[i], d_proj[:, :256])), i)
        add(acc2, 1, to_tiles(nn(normed_t_s[i], d_proj[:, 256:512])), i)

    def norm_backward(i):
        d_normed = d_normed_s[...]
        standard = standard_s[i]
        scaled = d_normed * gain
        inverse = inverse_s[i]
        inverse = jnp.concatenate([inverse, inverse], axis=1)
        d_input = inverse * (
            scaled
            - jnp.mean(scaled, axis=-1, keepdims=True)
            - standard * jnp.mean(scaled * standard, axis=-1, keepdims=True)
        )
        grad_win[rows_of(halves[i], HALF), :] = (hilbert_c[i] + d_input).astype(BF16)
        if i == 0:
            ex_grad[i] = to_side(i, grad_win, HALF, grad_win, 6)

    chunks = (
        (acc1, core_send1, core_recv1, m_send1, m_recv1, z_recv1, own_sum1),
        (acc2, core_send2, core_recv2, m_send2, m_recv2, z_recv2, own_sum2),
    )
    pers = (TILES // (n_x * n_y), TILES // (n_x * n_case))

    def sem(chunk, stage):
        return ar_send.at[chunk * 5 + stage], ar_recv.at[chunk * 5 + stage]

    def wait_total(ref, semaphore):
        pltpu.make_async_copy(ref, ref, semaphore).wait()

    def high_low(value):
        high = value.astype(BF16)
        low = (value - high.astype(F32)).astype(BF16)
        return jnp.concatenate([high, low], axis=0)

    def joined(tile):
        tile = tile.astype(F32)
        return tile[:8] + tile[8:]

    def core_start(chunk):
        acc, send, recv = chunks[chunk][:3]
        send[pl.ds(0, TILES)] = acc[1 - core].astype(BF16)
        if chunk:
            theirs = pl.multiple_of((1 - core) * 8, 8)
            send[TILES] = high_low(vector_s[pl.ds(theirs, 8), :])
        copy = remote(send, recv, *sem(chunk, 0), to_sib)
        copy.start()
        return copy

    def m_start(chunk, copy):
        acc, _, recv0, send, recv = chunks[chunk][:5]
        at, peers = planes[chunk]
        copy.wait()
        half = (acc[core] + recv0[pl.ds(0, TILES)].astype(F32)).astype(BF16)
        send[...] = half.reshape(len(peers) + 1, pers[chunk], 16, 128)
        recv[pl.ds(at, 1)] = send[pl.ds(at, 1)]
        s, r = sem(chunk, 1)
        for to, where in peers:
            remote(send.at[to], recv.at[at], s, r, where).start()

    def z_start(chunk):
        recv0, recv = chunks[chunk][4:6]
        at, peers = lines[chunk]
        wait_total(recv0.at[pl.ds(0, len(planes[chunk][1]))], sem(chunk, 1)[1])
        recv[at] = jnp.sum(recv0[...].astype(F32), axis=0).astype(BF16)
        s, r = sem(chunk, 2)
        slot = recv.at[at]
        for _, where in peers:
            remote(slot, slot, s, r, where).start()

    def m_back(chunk):
        recv0, result = chunks[chunk][5:7]
        at, peers = planes[chunk]
        wait_total(recv0.at[pl.ds(0, len(lines[chunk][1]))], sem(chunk, 2)[1])
        rows = pl.ds(at * pers[chunk], pers[chunk])
        result[rows] = jnp.sum(recv0[...].astype(F32), axis=0).astype(BF16)
        s, r = sem(chunk, 3)
        slot = result.at[rows]
        for _, where in peers:
            remote(slot, slot, s, r, where).start()

    def core_back(chunk):
        result = chunks[chunk][6]
        final = (sums1, sums2)[chunk].at[core]
        wait_total(result.at[pl.ds(0, len(planes[chunk][1]) * pers[chunk])], sem(chunk, 3)[1])
        copy = remote(result, final, *sem(chunk, 4), to_sib)
        copy.start()
        keep = pltpu.make_async_copy(result, final, local_sem.at[12 + chunk])
        keep.start()
        return copy, keep

    def vec_line_start():
        at, peers = lines[1]
        mine = pl.multiple_of(core * 8, 8)
        vec_z[at] = high_low(vector_s[pl.ds(mine, 8), :] + joined(core_recv2[TILES]))
        slot = vec_z.at[at]
        for _, where in peers:
            remote(slot, slot, ar_send.at[10], ar_recv.at[10], where).start()

    def vec_plane_start():
        at, peers = planes[1]
        count = len(lines[1][1])
        wait_total(vec_z.at[pl.ds(0, count)], ar_recv.at[10])
        total = joined(vec_z[0])
        for i in range(1, count + 1):
            total = total + joined(vec_z[i])
        vec_m[at] = high_low(total)
        slot = vec_m.at[at]
        for _, where in peers:
            remote(slot, slot, ar_send.at[11], ar_recv.at[11], where).start()

    def vec_back():
        wait_total(vec_m.at[pl.ds(0, len(planes[1][1]))], ar_recv.at[11])
        total = jnp.sum(vec_m[...].astype(F32), axis=0)
        own_sum2[TILES] = high_low(total[:8] + total[8:])

    def finish(chunk, copies):
        send1, _, recv2, result = chunks[chunk][3:7]
        count = len(planes[chunk][1])
        wait_total(send1.at[pl.ds(0, count)], sem(chunk, 1)[0])
        wait_total(recv2.at[pl.ds(0, len(lines[chunk][1]))], sem(chunk, 2)[0])
        wait_total(result.at[pl.ds(0, count * pers[chunk])], sem(chunk, 3)[0])
        for copy in copies:
            copy.wait()

    project(0)
    first_pass(0)
    block_output(0)
    project_cotangent(0)
    heard_rings()
    second_pass(0)
    forward_terms(0)
    backward_terms(0)
    norm_backward(0)
    project(1)
    first_pass(1)
    project_cotangent(1)
    second_pass(1)
    forward_terms(1)
    core_copy1 = core_start(0)
    backward_terms(1)
    core_copy2 = core_start(1)
    heard(len(steps) - 1, steps[-1])
    block_output(1)
    norm_backward(1)

    def to_z_order(pair, win, stage, result, at):
        for copy in pair:
            copy.wait_recv()
        for p in range(2):
            row = to_s[:, p * PATCH : (p + 1) * PATCH] - offset
            hot = one_hot(row, p * HALF, HALF + LEN)
            at_p = pl.ds(p * PATCH, PATCH)
            stage[at_p, :] = nn(hot, win[pl.ds(p * HALF, HALF + LEN), :]).astype(BF16)
        store = pltpu.make_async_copy(stage, result, local_sem.at[at])
        store.start()
        return store

    m_start(0, core_copy1)
    m_start(1, core_copy2)
    vec_line_start()
    ex_out[1] = to_side(1, out_win, HALF, out_win, 4)
    ex_grad[1] = to_side(1, grad_win, HALF, grad_win, 6)
    z_start(0)
    z_start(1)
    vec_plane_start()
    m_back(0)
    m_back(1)
    store_out = to_z_order(ex_out, out_win, out_stage, output, 10)
    store_grad = to_z_order(ex_grad, grad_win, grad_stage, grad_points, 11)
    vec_back()
    last1 = core_back(0)
    last2 = core_back(1)
    finish(0, last1)
    wait_total(vec_z.at[pl.ds(0, len(lines[1][1]))], ar_send.at[10])
    wait_total(vec_m.at[pl.ds(0, len(planes[1][1]))], ar_send.at[11])
    for pair in (ex_p, ex_c, ex_out, ex_grad):
        for copy in pair:
            copy.wait_send()
    store_out.wait()
    store_grad.wait()
    finish(1, last2)


def results_kernel(
    factor,
    output_in,
    grad_in,
    sums1_in,
    sums2_in,
    output,
    grad_points,
    grad_w_qkv,
    grad_b_qkv,
    grad_w_out,
    grad_b_out,
    grad_gain,
    grad_bias,
    output_s,
    grad_s,
    sums1,
    sums2,
    w_qkv_s,
    w_out_s,
    vec_s,
    in_sems,
    out_sems,
):
    loads = [(sums1_in, sums1), (sums2_in, sums2), (output_in, output_s), (grad_in, grad_s)]
    loads = [pltpu.make_async_copy(a, b, in_sems.at[i]) for i, (a, b) in enumerate(loads)]
    for load in loads:
        load.start()
    stores = []

    def store(a, b):
        stores.append(pltpu.make_async_copy(a, b, out_sems.at[len(stores)]))
        stores[-1].start()

    def block(sums, c, half):
        return sums[c, pl.ds(half * 16, 16)].reshape(256, 128).astype(F32) * factor

    def weight(sums, c, stage, first, result):
        for half in range(2):
            stage[:, pl.ds(first + half * 128, 128)] = block(sums, c, half)
        columns = pl.ds(first, D)
        store(stage.at[:, columns], result.at[:, columns])

    loads[0].wait()
    weight(sums1, 0, w_qkv_s, 512, grad_w_qkv)
    weight(sums1, 1, w_out_s, 0, grad_w_out)
    loads[1].wait()
    weight(sums2, 0, w_qkv_s, 0, grad_w_qkv)
    weight(sums2, 1, w_qkv_s, 256, grad_w_qkv)
    vectors = []
    for c in range(2):
        tile = sums2[c, TILES].astype(F32)
        vectors.append((tile[:8] + tile[8:]) * factor)
    for part in range(6):
        vec_s[0:1, part * 128 : part * 128 + 128] = vectors[0][part : part + 1]
        row = 1 + part // 2
        vec_s[row : row + 1, (part % 2) * 128 : (part % 2) * 128 + 128] = vectors[1][part : part + 1]
    store(vec_s.at[0], grad_b_qkv)
    store(vec_s.at[1, pl.ds(0, D)], grad_b_out)
    store(vec_s.at[2, pl.ds(0, D)], grad_gain)
    store(vec_s.at[3, pl.ds(0, D)], grad_bias)
    loads[2].wait()
    store(output_s, output)
    loads[3].wait()
    store(grad_s, grad_points)
    for copy in stores:
        copy.wait()


def on_device(n_pt, n_case, n_x, n_y, points, cotangent, to_hilbert, from_hilbert, *params):
    plane1, plane2 = n_x * n_y, n_x * n_case
    per1, per2 = TILES // plane1, TILES // plane2
    hbm = pl.BlockSpec(memory_space=pl.ANY)
    shape = jax.ShapeDtypeStruct
    rows = shape((LEN, D), BF16)

    def tiles(*lead):
        return pltpu.VMEM((*lead, 16, 128), BF16)

    output, grad_points, sums1, sums2 = pl.pallas_call(
        functools.partial(kernel, n_pt, n_case, n_x, n_y),
        out_shape=(
            rows,
            rows,
            shape((2, TILES, 16, 128), BF16),
            shape((2, TILES + 1, 16, 128), BF16),
        ),
        in_specs=[hbm] * 10,
        out_specs=(hbm,) * 4,
        scratch_shapes=[
            pltpu.VMEM((1, LEN), jnp.int32),
            pltpu.VMEM((1, LEN), jnp.int32),
            pltpu.VMEM((1, D), F32),
            pltpu.VMEM((1, D), F32),
            pltpu.VMEM((1, 3 * D), F32),
            pltpu.VMEM((1, D), F32),
            pltpu.VMEM((D, 3 * D), BF16),
            pltpu.VMEM((D, D), BF16),
            pltpu.VMEM((WIN, D), BF16),
            pltpu.VMEM((WIN, D), BF16),
            pltpu.VMEM((WIN, D), BF16),
            pltpu.VMEM((WIN, D), BF16),
            pltpu.VMEM((2, PATCH, D), F32),
            pltpu.VMEM((2, PATCH, D), F32),
            pltpu.VMEM((2, PATCH, D), F32),
            pltpu.VMEM((2, PATCH, 128), F32),
            pltpu.VMEM((2, D, PATCH), BF16),
            pltpu.VMEM((2, PATCH, 3 * D), BF16),
            pltpu.VMEM((2, PATCH, D), BF16),
            pltpu.VMEM((8, PATCH, PATCH), F32),
            pltpu.VMEM((2, D, PATCH), BF16),
            pltpu.VMEM((2, PATCH, 3 * D), BF16),
            pltpu.VMEM((PATCH, D), F32),
            pltpu.VMEM((16, 128), F32),
            pltpu.VMEM((2, TILES, 16, 128), F32),
            pltpu.VMEM((2, TILES, 16, 128), F32),
            tiles(TILES),
            tiles(TILES + 1),
            tiles(TILES),
            tiles(TILES + 1),
            tiles(plane1, per1),
            tiles(plane2, per2),
            tiles(plane1, per1),
            tiles(plane2, per2),
            tiles(n_case, per1),
            tiles(n_y, per2),
            tiles(n_y),
            tiles(plane2),
            tiles(TILES),
            tiles(TILES + 1),
            pltpu.VMEM((LEN, D), BF16),
            pltpu.VMEM((LEN, D), BF16),
            pltpu.SemaphoreType.DMA((14,)),
            pltpu.SemaphoreType.DMA((8,)),
            pltpu.SemaphoreType.DMA((8,)),
            pltpu.SemaphoreType.DMA((14,)),
            pltpu.SemaphoreType.DMA((14,)),
            pltpu.SemaphoreType.REGULAR((3,)),
        ],
        compiler_params=pltpu.CompilerParams(
            collective_id=0, has_side_effects=True, vmem_limit_bytes=VMEM_LIMIT
        ),
    )(points[0], cotangent[0], to_hilbert, from_hilbert, *params)
    factor = 1.0 / math.sqrt(n_pt * n_case * LEN)
    result = pl.pallas_call(
        functools.partial(results_kernel, factor),
        out_shape=(
            rows,
            rows,
            shape((D, 3 * D), F32),
            shape((3 * D,), F32),
            shape((D, D), F32),
            shape((D,), F32),
            shape((D,), F32),
            shape((D,), F32),
        ),
        in_specs=[hbm] * 4,
        out_specs=(hbm,) * 8,
        scratch_shapes=[
            pltpu.VMEM((LEN, D), BF16),
            pltpu.VMEM((LEN, D), BF16),
            tiles(2, TILES),
            tiles(2, TILES + 1),
            pltpu.VMEM((D, 3 * D), F32),
            pltpu.VMEM((D, D), F32),
            pltpu.VMEM((4, 3 * D), F32),
            pltpu.SemaphoreType.DMA((4,)),
            pltpu.SemaphoreType.DMA((10,)),
        ],
        compiler_params=pltpu.CompilerParams(vmem_limit_bytes=VMEM_LIMIT),
    )(output, grad_points, sums1, sums2)
    return (result[0][None], result[1][None], *result[2:])


def solution(mesh):
    n_pt, n_case = mesh.shape["pt"], mesh.shape["case"]
    members = n_pt // 2
    n_y = 8 if members >= 32 else 2
    rows = P("case", "pt", None)
    index = P("case", "pt")
    return jax.shard_map(
        functools.partial(on_device, n_pt, n_case, members // n_y, n_y),
        mesh=mesh,
        in_specs=(rows, rows, index, index) + (P(),) * 6,
        out_specs=(rows, rows) + (P(),) * 6,
        check_vma=False,
    )
```
